256 devices in a mesh: ctx: 32 (over x, y, core), tp: 8 (over z).
Axes of the slice: x: 4, y: 4, z: 8, core: 2. Of those that a mesh axis runs over, the one named last changes fastest.
Arguments:
- queries: bfloat16 [4096, 128, 576], P('ctx', 'tp'), may hold values from -73 to 73
- latent_block_cache: bfloat16 [512, 128, 576], P('ctx'), may hold values from -12 to 12
- selected_block_lists: int32 [4096, 4], P('ctx'), may hold values from 0 to 511, as said below
- output_gradient: bfloat16 [4096, 7168], P(None, 'ctx'), may hold values from -6 to 6
- output_weight: bfloat16 [16384, 7168], P('tp', 'ctx'), may hold values from -0.046875 to 0.046875
- adapter_down: bfloat16 [32, 16384], P(None, 'tp'), may hold values from -0.046875 to 0.046875
- adapter_up: bfloat16 [32, 7168], P(None, 'ctx'), may hold values from -0.119628906 to 0.119628906
- value_up_map: bfloat16 [128, 512, 128], P('tp'), may hold values from -0.25 to 0.25
- saved_head_input: bfloat16 [4096, 16384], P('ctx', 'tp'), may hold values from -6 to 6
Outputs:
- query_grads: bfloat16 [4096, 128, 576], P('ctx', 'tp')
- cache_grads: float32 [512, 128, 576], P('ctx', 'tp')
- down_gradient: float32 [32, 16384], P(None, 'tp')
- up_gradient: float32 [32, 7168], P(None, 'ctx')
The draws below stay inside these ranges and needn't reach their ends.
Inputs may be any that keep to these rules, and one draw needn't show every extreme that they name: `selected_block_lists`: each query names 4 different blocks. The queries of one ctx index fall into 2 equal groups of consecutive queries; each group names exactly 6 distinct blocks together, and different groups of one ctx index name different blocks, so that the ctx index names exactly 12. At most 1 of them lie among the 16 blocks held by one ctx index, and the last ctx index gives exactly 1 to every ctx index.
All inputs are finite; a program needn't handle non-finite values.
Results may differ from the reference program's by a relative error of at most 0.04.
Values may be sent and summed in bfloat16 or wider, within the bound.
No kernel may reach another device: no remote copies, remote signals or barrier semaphores. Data moves between devices by JAX's collectives and lax.ppermute only.
A program may use at most 192 MiB of HBM per device.

```python
import math
import jax
import jax.numpy as jnp
from jax import lax

HEADS = 128
DL = 512
DV = 128
MODEL_WIDTH = 7168
ADAPTER_RANK = 32
BLK = 128
TOPB = 4
GCANDS = 6
QGROUPS = 2
QRY_DEV = 128
BLK_DEV = 16
CANDS = 12
DK = 576
PROJECTION_WIDTH = 16384
QUERIES = 4096
BLOCKS = 512
CAP = 1
N_CTX = 32


def pick_lists(key):

    def one_device(device_key):
        owner_key, other_key, order_key, query_key = jax.random.split(device_key, 4)
        recent = (BLOCKS - 1 - jnp.arange(CAP)).astype(jnp.int32)
        sink = jnp.zeros((1,), jnp.int32)
        owner_keys = jax.random.split(owner_key, N_CTX - 1)
        local_ids = jax.vmap(lambda one_key: jax.random.permutation(one_key, BLK_DEV - 1)[:CAP] + 1)(owner_keys)
        pairs = (jnp.arange(N_CTX - 1, dtype=jnp.int32)[:, None] * BLK_DEV + local_ids).reshape(-1).astype(jnp.int32)
        others = pairs[1 + jax.random.permutation(other_key, (N_CTX - 1) * CAP - 1)[:CANDS - CAP - 1]]
        candidates = jnp.concatenate([sink, recent, others])[jax.random.permutation(order_key, CANDS)]
        query_keys = jax.random.split(query_key, QRY_DEV)
        picks = jax.vmap(lambda one_key: jax.random.permutation(one_key, GCANDS)[:TOPB])(query_keys)
        per_group = QRY_DEV // QGROUPS
        positions = jnp.arange(QRY_DEV, dtype=jnp.int32)
        local_pos = (positions % per_group)[:, None]
        group_base = (positions // per_group)[:, None] * GCANDS
        first_rows = jnp.arange(TOPB, dtype=jnp.int32)[None, :]
        second_rows = GCANDS - TOPB + first_rows
        picks = jnp.where(local_pos == 0, first_rows, jnp.where(local_pos == 1, second_rows, picks))
        picks = picks + group_base
        return candidates[picks].astype(jnp.int32)
    device_keys = jax.random.split(jax.random.fold_in(key, 11), N_CTX)
    return jax.vmap(one_device)(device_keys).reshape(QUERIES, TOPB)


def draw_selected_block_lists(key, part):
    return pick_lists(key)


def draw_queries(key, part):
    key = jax.random.fold_in(key, 3)
    result = jnp.clip(jax.random.normal(key, (QUERIES, HEADS, DK), jnp.float32), -6.0, 6.0)
    return result.astype(jnp.bfloat16)


def draw_latent_block_cache(key, part):
    key = jax.random.fold_in(key, 5)
    result = jnp.clip(jax.random.normal(key, (BLOCKS, BLK, DK), jnp.float32), -6.0, 6.0)
    return result.astype(jnp.bfloat16)


def strengthened(array, key, source, target, shards_of, factor):
    owner, partner = [(jnp.arange(array.shape[dim]) // (array.shape[dim] // shards_of)).reshape([-1 if axis == dim else 1 for axis in range(array.ndim)]) for dim in (source, target)]
    chosen = jax.random.permutation(key, shards_of)[partner]
    strong = (owner == chosen) | (owner == (partner + shards_of // 2) % shards_of)
    return jnp.where(strong, factor * array, array)


def block_scale(key, dims, shards, least, high):
    def one(dim, parts):
        steps = jax.random.uniform(jax.random.fold_in(jax.random.fold_in(key, 6), dim), (parts,), jnp.float32, least / len(shards), high / len(shards))
        return jnp.repeat(jnp.exp(steps), dims[dim] // parts).reshape((-1,) + (1,) * (len(dims) - dim - 1))

    level = one(*shards[0])
    for cut in shards[1:]:
        level = level * one(*cut)
    return level


def bell_draw(stream_key, shape, scale, bound, cuts=(), kind=jnp.bfloat16):
    entries = scale * jax.random.normal(stream_key, shape, jnp.float32)
    if cuts:
        entries = entries * block_scale(stream_key, shape, cuts, -0.22, 0.18)
    return jnp.clip(entries, -bound, bound).astype(kind)


def noise_with(rng, extent, scale, most, cuts, heavy, kind=jnp.bfloat16):
    drawn = scale * jax.random.normal(rng, extent, jnp.float32)
    if cuts:
        drawn = drawn * block_scale(rng, extent, cuts, -0.22, 0.18)
    return jnp.clip(strengthened(drawn, jax.random.fold_in(rng, 3), *heavy), -most, most).astype(kind)


def setup_inputs(seed: int = 0) -> dict:
    keys = jax.random.split(jax.random.key(seed), 10)
    return {
        "queries": draw_queries(jax.random.fold_in(keys[9], 71), 0),
        "latent_block_cache": draw_latent_block_cache(jax.random.fold_in(keys[9], 71), 0),
        "selected_block_lists": draw_selected_block_lists(jax.random.fold_in(keys[9], 71), 0),
        "output_gradient": noise_with(keys[3], (QUERIES, MODEL_WIDTH), 1.0, 6.0, ((1, 32),), (1, 0, 32, 2.75)),
        "output_weight": bell_draw(keys[4], (PROJECTION_WIDTH, MODEL_WIDTH), PROJECTION_WIDTH ** -0.5, 0.046875, ((0, 8), (1, 32))),
        "adapter_down": bell_draw(keys[5], (ADAPTER_RANK, PROJECTION_WIDTH), PROJECTION_WIDTH ** -0.5, 0.046875, ((1, 8),)),
        "adapter_up": bell_draw(keys[6], (ADAPTER_RANK, MODEL_WIDTH), 0.02, 0.119628906, ((1, 32),)),
        "value_up_map": bell_draw(keys[7], (HEADS, DL, DV), DL ** -0.5, 0.25, ((0, 8),)),
        "saved_head_input": bell_draw(keys[8], (QUERIES, PROJECTION_WIDTH), 1.0, 6.0, ((0, 32), (1, 8))),
    }


SCORE_SCALE = 192.0 ** -0.5
ADAPTER_SCALE = 2.0


def reference(queries, latent_block_cache, selected_block_lists, output_gradient, output_weight, adapter_down, adapter_up, value_up_map, saved_head_input):
    column_width = MODEL_WIDTH // N_CTX
    gradient_columns = jnp.moveaxis(output_gradient.reshape(QUERIES, N_CTX, column_width), 1, 0)
    weight_columns = jnp.moveaxis(output_weight.reshape(PROJECTION_WIDTH, N_CTX, column_width), 1, 0)
    up_columns = jnp.moveaxis(adapter_up.reshape(ADAPTER_RANK, N_CTX, column_width), 1, 0)
    down_single_float = adapter_down.astype(jnp.float32)

    def addition_piece(running_total, pieces):
        head_overall_total, adapter_total = running_total
        grad_piece, weight_piece, up_piece = pieces
        low_rank_part = jnp.dot(grad_piece, up_piece.T, preferred_element_type=jnp.float32)
        term_portion = jnp.dot(grad_piece, weight_piece.T, preferred_element_type=jnp.float32)
        term_portion = term_portion + ADAPTER_SCALE * jnp.dot(low_rank_part, down_single_float, precision=lax.Precision.HIGHEST)
        term_rounded = lax.optimization_barrier(term_portion.astype(jnp.bfloat16)).astype(jnp.float32)
        low_rank_rounded = lax.optimization_barrier(low_rank_part.astype(jnp.bfloat16)).astype(jnp.float32)
        return (head_overall_total + term_rounded, adapter_total + low_rank_rounded), None

    initial_sums = (jnp.zeros((QUERIES, PROJECTION_WIDTH), jnp.float32), jnp.zeros((QUERIES, ADAPTER_RANK), jnp.float32))
    (head_summed_total, adapter_sum), unused_result = lax.scan(addition_piece, initial_sums, (gradient_columns, weight_columns, up_columns))
    head_grads = head_summed_total.astype(jnp.bfloat16)
    adapter_gradient = (ADAPTER_SCALE * adapter_sum).astype(jnp.bfloat16)
    adapter_rows = jnp.dot(saved_head_input, adapter_down.T, preferred_element_type=jnp.float32).astype(jnp.bfloat16)
    up_gradient = ADAPTER_SCALE * jnp.dot(adapter_rows.T, output_gradient, preferred_element_type=jnp.float32)
    down_gradient = jnp.dot(adapter_gradient.T, saved_head_input, preferred_element_type=jnp.float32)
    out_grads = jnp.einsum('qhv,hlv->qhl', head_grads.reshape(QUERIES, HEADS, DV).astype(jnp.float32),
                           value_up_map.astype(jnp.float32)).astype(jnp.bfloat16)

    group_size = math.gcd(QUERIES, 8)
    steps_count = QUERIES // group_size
    cache_rows = latent_block_cache.reshape(BLOCKS * BLK, DK)
    offsets = jnp.arange(BLK, dtype=jnp.int32)

    def attend(grad_rows, pieces):
        query_piece, grad_piece, list_piece = pieces
        row_index = (list_piece[:, :, None] * BLK + offsets[None, None, :]).reshape(group_size, TOPB * BLK)
        key_rows = cache_rows[row_index].astype(jnp.float32)
        query_float = query_piece.astype(jnp.float32)
        grad_float = grad_piece.astype(jnp.float32)
        scores = SCORE_SCALE * jnp.einsum('ghk,gsk->ghs', query_float, key_rows)
        highest = jnp.max(scores, axis=2, keepdims=True)
        weights = jnp.exp(scores - highest)
        weights = weights / jnp.sum(weights, axis=2, keepdims=True)
        weights_round = lax.optimization_barrier(weights.astype(jnp.bfloat16)).astype(jnp.float32)
        prob_grads = jnp.einsum('ghl,gsl->ghs', grad_float, key_rows[:, :, :DL])
        row_delta = jnp.sum(weights * prob_grads, axis=2, keepdims=True)
        score_grads = (weights * (prob_grads - row_delta) * SCORE_SCALE).astype(jnp.bfloat16)
        score_grads = lax.optimization_barrier(score_grads).astype(jnp.float32)
        query_out = jnp.einsum('ghs,gsk->ghk', score_grads, key_rows).astype(jnp.bfloat16)
        key_grads = jnp.einsum('ghs,ghk->gsk', score_grads, query_float)
        latent_part = key_grads[:, :, :DL] + jnp.einsum('ghs,ghl->gsl', weights_round, grad_float)
        key_grads = jnp.concatenate([latent_part, key_grads[:, :, DL:]], axis=2)
        grad_rows = grad_rows.at[row_index.reshape(-1)].add(key_grads.reshape(group_size * TOPB * BLK, DK))
        return grad_rows, query_out

    pieces = (queries.reshape(steps_count, group_size, HEADS, DK),
              out_grads.reshape(steps_count, group_size, HEADS, DL),
              selected_block_lists.reshape(steps_count, group_size, TOPB))
    grad_rows, query_grads = lax.scan(attend, jnp.zeros((BLOCKS * BLK, DK), jnp.float32), pieces)
    return (query_grads.reshape(QUERIES, HEADS, DK), grad_rows.reshape(BLOCKS, BLK, DK), down_gradient, up_gradient)
```

```python
import functools

import jax
import jax.numpy as jnp
from jax import lax
from jax.experimental import pallas as pl
from jax.experimental.pallas import tpu as pltpu
from jax.sharding import Mesh, PartitionSpec as P

SCORE_SCALE = 192.0 ** (-0.5)
ADAPTER_SCALE = 2.0

NX = 4
NY = 4
NCORE = 2
NCTX = 32
NTP = 8
GROUPS = 2
GSLOTS = 6
SLOTS = 12
BLOCK = 128
WIDTH = 576
LATENT = 512
VALUE = 128
HEADS_DEV = 16
QRY_DEV = 128
GQ = 64
RANK = 32
FEATS = 224
HEAD_IN = 2048
PIECE = BLOCK // NTP
SLOT_LANES = 896
GROUP_ROWS = GSLOTS * BLOCK
MASKED = -1e30

bf16 = jnp.bfloat16
f32 = jnp.float32

NN = (((1,), (0,)), ((), ()))
NT = (((1,), (1,)), ((), ()))
TN = (((0,), (0,)), ((), ()))


def mm(a, b, dims):
    return lax.dot_general(a, b, dims, preferred_element_type=f32)


def params(mib):
    return pltpu.CompilerParams(vmem_limit_bytes=mib * 1024 * 1024)


def cost(flops, nbytes):
    return pl.CostEstimate(flops=int(flops), bytes_accessed=int(nbytes), transcendentals=0)


def smem():
    return pl.BlockSpec(memory_space=pltpu.SMEM)


def vmem():
    return pl.BlockSpec(memory_space=pltpu.VMEM)


def prep_kernel(place, g_ref, up_ref, w_ref, down_ref, mine, other, low_out, wcat, turned):
    step = pl.program_id(0)
    core = place[2]
    tp = place[3]

    @pl.when(step == 0)
    def _():
        wcat[:FEATS, :] = w_ref[...]
        wcat[FEATS:, :] = (ADAPTER_SCALE * down_ref[...].astype(f32)).astype(bf16)

    g = g_ref[...]
    low = mm(up_ref[...], g, NN).astype(bf16)
    turned[...] = jnp.concatenate([g, low], axis=0).T
    mine[0] = turned[pl.ds(pl.multiple_of(core * QRY_DEV, QRY_DEV), QRY_DEV), :]
    other[0] = turned[pl.ds(pl.multiple_of((1 - core) * QRY_DEV, QRY_DEV), QRY_DEV), :]
    for half in range(2):
        start = pl.multiple_of(half * QRY_DEV + tp * PIECE, PIECE)
        low_out[half] = turned[pl.ds(start, PIECE), 128:]


def prep(place, g_t, up, w_t, down):
    pairs = NX * NY
    return pl.pallas_call(
        prep_kernel,
        grid_spec=pltpu.PrefetchScalarGridSpec(
            num_scalar_prefetch=1,
            grid=(pairs,),
            in_specs=[
                pl.BlockSpec((FEATS, 2 * QRY_DEV), lambda s, p: (0, s)),
                pl.BlockSpec((RANK, FEATS), lambda s, p: (0, 0)),
                pl.BlockSpec((FEATS, HEAD_IN), lambda s, p: (0, 0)),
                pl.BlockSpec((RANK, HEAD_IN), lambda s, p: (0, 0)),
            ],
            out_specs=[
                pl.BlockSpec((1, QRY_DEV, 256), lambda s, p: (s, 0, 0)),
                pl.BlockSpec((1, QRY_DEV, 256), lambda s, p: (s, 0, 0)),
                pl.BlockSpec((2, PIECE, 128), lambda s, p: (s, 0, 0)),
                pl.BlockSpec((256, HEAD_IN), lambda s, p: (0, 0)),
            ],
            scratch_shapes=[pltpu.VMEM((256, 256), bf16)],
        ),
        out_shape=[
            jax.ShapeDtypeStruct((pairs, QRY_DEV, 256), bf16),
            jax.ShapeDtypeStruct((pairs, QRY_DEV, 256), bf16),
            jax.ShapeDtypeStruct((NCTX, PIECE, 128), bf16),
            jax.ShapeDtypeStruct((256, HEAD_IN), bf16),
        ],
        compiler_params=params(24),
        cost_estimate=cost(1e8, 6e6),
    )(place, g_t, up, w_t, down)


def head_kernel(place, m0, m1, p0, p1, w_own, w_pair, *outs):
    (a_own, a_p1, a_m1, a_p2, a_m2, b_own, b_p1, b_m1, b_p2, b_m2) = outs
    step = pl.program_id(0)
    own = jnp.concatenate([m0[0], m1[0]], axis=0)
    pair = jnp.concatenate([p0[0], p1[0]], axis=0)
    half = HEAD_IN // 2
    for part in range(2):
        cols = slice(part * half, (part + 1) * half)
        both = mm(own, w_own[:, cols], NN) + mm(pair, w_pair[:, cols], NN)
        both = both.astype(bf16)
        group_a = [both[0:GQ], both[2 * GQ : 3 * GQ]]
        group_b = [both[GQ : 2 * GQ], both[3 * GQ : 4 * GQ]]
        a_steps = {0: a_own, 1: a_own, 2: a_p2, 3: a_p1, 4: a_p1, 5: a_m1, 6: a_m1, 7: a_m2}
        for number, ref in a_steps.items():

            @pl.when(step == number)
            def _(ref=ref):
                ref[0, :, cols] = group_a[0]
                ref[1, :, cols] = group_a[1]

        b_steps = [
            (b_own, b_p2),
            (b_p1, b_m1),
            (b_own, b_p2),
            (b_p1, b_m1),
            (b_own, b_p1),
            (b_m1, b_m2),
            (b_own, b_p1),
            (b_m1, b_m2),
        ]
        for number, refs in enumerate(b_steps):

            @pl.when(step == number)
            def _(refs=refs):
                refs[0][0, :, cols] = group_b[0]
                refs[1][0, :, cols] = group_b[1]


def head_partials(place, mine, theirs, w_own, w_pair):
    def row(number):
        def index(s, p):
            x = lax.rem(p[0] + s // 2, NX)
            y = lax.rem(p[1] + 2 * lax.rem(s, 2) + number, NY)
            return (x * NY + y, 0, 0)

        return pl.BlockSpec((1, QRY_DEV, 256), index)

    def whole():
        return pl.BlockSpec((256, HEAD_IN), lambda s, p: (0, 0))

    def past(s, *bounds):
        total = 0
        for b in bounds:
            total = total + (s > b).astype(jnp.int32)
        return total

    def out(count, block, index):
        return (
            pl.BlockSpec((block, GQ, HEAD_IN), lambda s, p: (index(s), 0, 0)),
            jax.ShapeDtypeStruct((count, GQ, HEAD_IN), bf16),
        )

    outs = [
        out(4, 2, lambda s: past(s, 0)),
        out(4, 2, lambda s: past(s, 3)),
        out(4, 2, lambda s: past(s, 5)),
        out(2, 2, lambda s: 0),
        out(2, 2, lambda s: 0),
        out(4, 1, lambda s: past(s, 1, 3, 5)),
        out(4, 1, lambda s: past(s, 1, 3, 4)),
        out(4, 1, lambda s: past(s, 1, 3, 5)),
        out(2, 1, lambda s: past(s, 0)),
        out(2, 1, lambda s: past(s, 5)),
    ]
    return pl.pallas_call(
        head_kernel,
        grid_spec=pltpu.PrefetchScalarGridSpec(
            num_scalar_prefetch=1,
            grid=(8,),
            in_specs=[row(0), row(1), row(0), row(1), whole(), whole()],
            out_specs=[o[0] for o in outs],
        ),
        out_shape=[o[1] for o in outs],
        compiler_params=params(32),
        cost_estimate=cost(4.3e9, 13e6),
    )(place, mine, mine, theirs, theirs, w_own, w_pair)


def shift(value, axis, size, by):
    return lax.ppermute(value, axis, [(i, (i + by) % size) for i in range(size)])


def add(*terms):
    total = terms[0].astype(f32)
    for t in terms[1:]:
        total = total + t.astype(f32)
    return total.astype(bf16)


def ring_first(axis, own, plus1, minus1, plus2, minus2):
    from_minus = shift(plus1, axis, 4, 1)
    from_plus = shift(minus1, axis, 4, -1)
    return from_minus, from_plus


def reduce_second(axis, total):
    h = GQ // 2
    p1 = jnp.concatenate([total[2][:h], total[1][h:]], axis=0)
    m1 = jnp.concatenate([total[2][h:], total[3][:h]], axis=0)
    from_minus = shift(p1, axis, 4, 1)
    from_plus = shift(m1, axis, 4, -1)
    p2 = add(total[1][:h], from_minus[:h])
    m2 = add(total[3][h:], from_plus[:h])
    last_minus = shift(p2, axis, 4, 1)
    last_plus = shift(m2, axis, 4, -1)
    top = add(total[0][:h], from_plus[h:], last_minus)
    low = add(total[0][h:], from_minus[h:], last_plus)
    return jnp.concatenate([top, low], axis=0)


def turn_kernel(place, cache_ref, out_ref, turned):
    start = pl.multiple_of(place[3] * PIECE, PIECE)
    for b in range(cache_ref.shape[0]):
        turned[...] = cache_ref[b].T
        out_ref[b] = turned[pl.ds(start, PIECE), :]


def turn_cache(place, cache_t):
    blocks = cache_t.shape[0]
    return pl.pallas_call(
        turn_kernel,
        in_specs=[smem(), vmem()],
        out_specs=vmem(),
        out_shape=jax.ShapeDtypeStruct((blocks, PIECE, WIDTH), bf16),
        scratch_shapes=[pltpu.VMEM((BLOCK, WIDTH), bf16)],
        compiler_params=params(16),
        cost_estimate=cost(1e6, 3e6),
    )(place, cache_t)


def rows_kernel(saved_ref, down_ref, out_ref):
    rows_t = mm(down_ref[...], saved_ref[...], NT).astype(bf16)
    out_ref[:, :128] = rows_t[:16]
    out_ref[:, 128:] = rows_t[16:]


def adapter_rows(saved, down):
    return pl.pallas_call(
        rows_kernel,
        in_specs=[vmem(), vmem()],
        out_specs=vmem(),
        out_shape=jax.ShapeDtypeStruct((16, 256), bf16),
        compiler_params=params(8),
        cost_estimate=cost(1.7e7, 7e5),
    )(saved, down)


def serve_kernel(ids, cache_ref, low_ref, rows_ref, out_ref):
    lane = lax.broadcasted_iota(jnp.int32, (PIECE, 128), 1)
    rows = rows_ref[...]
    for s in range(NCTX):
        block = cache_ref[ids[s]]
        out_ref[s, :, :512] = block[:, :512]
        out_ref[s, :, 512:640] = low_ref[s]
        out_ref[s, :, 512:576] = block[:, 512:]
        out_ref[s, :, 640:] = rows


def serve(ids, cache_piece, low, rows):
    return pl.pallas_call(
        serve_kernel,
        in_specs=[smem(), vmem(), vmem(), vmem()],
        out_specs=vmem(),
        out_shape=jax.ShapeDtypeStruct((NCTX, PIECE, SLOT_LANES), bf16),
        compiler_params=params(8),
        cost_estimate=cost(1e6, 2e6),
    )(ids, cache_piece, low, rows)


def pick_kernel(chosen, got_ref, g_ref, out_ref, rows_all):
    for k in range(SLOTS):
        out_ref[k * PIECE : (k + 1) * PIECE, :] = got_ref[chosen[k], :, :WIDTH]
    low = got_ref[0, :, 512:640].astype(f32)
    for s in range(1, NCTX):
        low = low + got_ref[s, :, 512:640].astype(f32)
    for s in range(NCTX):
        rows_all[0:16, s * 128 : (s + 1) * 128] = got_ref[s, :, 640:768]
        rows_all[16:32, s * 128 : (s + 1) * 128] = got_ref[s, :, 768:896]
    up = mm(rows_all[...], g_ref[...], NT).astype(bf16)
    base = SLOTS * PIECE
    out_ref[base : base + 16, :] = jnp.zeros((16, WIDTH), bf16)
    out_ref[base : base + 16, 384:512] = low.astype(bf16)
    out_ref[base : base + 16, :FEATS] = up[:16]
    out_ref[base : base + 16, 256 : 256 + FEATS] = up[16:]


def pick(chosen, got, g_t):
    return pl.pallas_call(
        pick_kernel,
        in_specs=[smem(), vmem(), vmem()],
        out_specs=vmem(),
        out_shape=jax.ShapeDtypeStruct((SLOTS * PIECE + 16, WIDTH), bf16),
        scratch_shapes=[pltpu.VMEM((RANK, NCTX * QRY_DEV), bf16)],
        compiler_params=params(16),
        cost_estimate=cost(6e7, 3e6),
    )(chosen, got, g_t)


def gather_tp(own):
    pieces = [None] * NTP
    pieces[0] = own
    forward = own
    back = own
    for step in range(1, 5):
        forward = shift(forward, "tp", NTP, -1)
        pieces[step] = forward
        if step < 4:
            back = shift(back, "tp", NTP, 1)
            pieces[NTP - step] = back
    return pieces


def adapter_kernel(place, *refs):
    pieces = refs[:NTP]
    saved_ref, down_out, up_out, low = refs[NTP:]
    base = SLOTS * PIECE
    total = jnp.zeros((16, 512), f32)
    for d in range(NTP):
        rows = pieces[d][base : base + 16, :512]
        total = total + rows.astype(f32)
        where = lax.rem(place[3] + d, NTP)
        low[pl.ds(pl.multiple_of(where * PIECE, PIECE), PIECE), :] = rows[:, 384:]
    up_out[:16, :] = ADAPTER_SCALE * total[:, :FEATS]
    up_out[16:, :] = ADAPTER_SCALE * total[:, 256 : 256 + FEATS]
    grads = mm(low[...], saved_ref[...], TN)
    down_out[...] = (ADAPTER_SCALE * grads[96:, :]).astype(bf16)


def adapter_grads(place, pieces, saved):
    return pl.pallas_call(
        adapter_kernel,
        in_specs=[smem()] + [vmem()] * (NTP + 1),
        out_specs=[vmem(), vmem()],
        out_shape=[
            jax.ShapeDtypeStruct((RANK, HEAD_IN), bf16),
            jax.ShapeDtypeStruct((RANK, FEATS), f32),
        ],
        scratch_shapes=[pltpu.VMEM((QRY_DEV, 128), bf16)],
        compiler_params=params(16),
        cost_estimate=cost(7e7, 3e6),
    )(place, *pieces, saved)


def attend_kernel(*refs):
    pieces = refs[:NTP]
    q_ref, hg_a, hg_b, vu_ref, bias_ref, dq_ref = refs[NTP : NTP + 6]
    outs = refs[NTP + 6 : NTP + 15]
    keys, keys_t, acc, spread = refs[NTP + 15 :]
    step = pl.program_id(0)
    span = GSLOTS * PIECE

    @pl.when(step == 0)
    def _():
        for g in range(GROUPS):
            for d in range(NTP):
                keys[g, d * span : (d + 1) * span, :] = pieces[d][g * span : (g + 1) * span, :]
            keys_t[g] = keys[g].T
        acc[...] = jnp.zeros_like(acc)
        spread[...] = jnp.zeros_like(spread)

    maps = jnp.concatenate([vu_ref[h] for h in range(4)], axis=1)
    dqs = []
    for g in range(GROUPS):
        hg = (hg_a, hg_b)[g]
        q4 = jnp.concatenate([q_ref[h][:, g * GQ : (g + 1) * GQ] for h in range(4)], axis=1)
        for h in range(4):
            spread[h * GQ : (h + 1) * GQ, h * VALUE : (h + 1) * VALUE] = hg[
                :, h * VALUE : (h + 1) * VALUE
            ]
        og = mm(maps, spread[...], NT).astype(bf16)
        s = mm(keys[g], q4, NN)
        s = s.reshape(NTP, GSLOTS, PIECE, 4 * GQ) * SCORE_SCALE + bias_ref[g][None, :, None, :]
        s = s.reshape(GROUP_ROWS, 4 * GQ)
        top = jnp.max(s, axis=0, keepdims=True)
        p = jnp.exp(s - top)
        p = p * (1.0 / jnp.sum(p, axis=0, keepdims=True))
        dp = mm(keys[g, :, :LATENT], og, NN)
        delta = jnp.sum(p * dp, axis=0, keepdims=True)
        ds = (p * (dp - delta) * SCORE_SCALE).astype(bf16)
        dqs.append(mm(keys_t[g], ds, NN).astype(bf16))
        acc[g] += mm(ds, q4, NT)
        acc[g, :, :LATENT] += mm(p.astype(bf16), og, NT)
    for h in range(4):
        cols = slice(h * GQ, (h + 1) * GQ)
        dq_ref[h] = jnp.concatenate([dqs[0][:, cols], dqs[1][:, cols]], axis=1)

    @pl.when(step == pl.num_programs(0) - 1)
    def _():
        for d in range(NTP):
            for g in range(GROUPS):
                rows = acc[g, d * span : (d + 1) * span, :].astype(bf16)
                if d < 4:
                    outs[d][g * span : (g + 1) * span, :] = rows
                elif d == 4:
                    outs[4 + g][...] = rows
                else:
                    outs[d + 1][g * span : (g + 1) * span, :] = rows


def attend(pieces, q_t, hg_a, hg_b, vu, bias):
    span = GSLOTS * PIECE
    whole = lambda s: (0, 0)
    rows = [2 * span] * 4 + [span] * 2 + [2 * span] * 3
    out_specs = [pl.BlockSpec((4, WIDTH, QRY_DEV), lambda s: (s, 0, 0))]
    out_specs += [pl.BlockSpec((r, WIDTH), whole) for r in rows]
    out_shape = [jax.ShapeDtypeStruct((HEADS_DEV, WIDTH, QRY_DEV), bf16)]
    out_shape += [jax.ShapeDtypeStruct((r, WIDTH), bf16) for r in rows]
    return pl.pallas_call(
        attend_kernel,
        grid=(HEADS_DEV // 4,),
        in_specs=[pl.BlockSpec(pieces[0].shape, whole)] * NTP
        + [
            pl.BlockSpec((4, WIDTH, QRY_DEV), lambda s: (s, 0, 0)),
            pl.BlockSpec((GQ, 4 * VALUE), lambda s: (0, s)),
            pl.BlockSpec((GQ, 4 * VALUE), lambda s: (0, s)),
            pl.BlockSpec((4, LATENT, VALUE), lambda s: (s, 0, 0)),
            pl.BlockSpec(bias.shape, lambda s: (0, 0, 0)),
        ],
        out_specs=out_specs,
        out_shape=out_shape,
        scratch_shapes=[
            pltpu.VMEM((GROUPS, GROUP_ROWS, WIDTH), bf16),
            pltpu.VMEM((GROUPS, WIDTH, GROUP_ROWS), bf16),
            pltpu.VMEM((GROUPS, GROUP_ROWS, WIDTH), f32),
            pltpu.VMEM((4 * GQ, 4 * VALUE), bf16),
        ],
        compiler_params=params(48),
        cost_estimate=cost(1e10, 1.2e7),
    )(*pieces, q_t, hg_a, hg_b, vu, bias)


def reduce_tp(parts):
    d0, d1, d2, d3, d4a, d4b, d5, d6, d7 = parts
    half = d4a.shape[0]
    up = shift(d4a, "tp", NTP, 1)
    down = shift(d4b, "tp", NTP, -1)
    up = shift(jnp.concatenate([add(d3[:half], up), d3[half:]], axis=0), "tp", NTP, 1)
    down = shift(jnp.concatenate([d5[:half], add(d5[half:], down)], axis=0), "tp", NTP, -1)
    up = shift(add(d2, up), "tp", NTP, 1)
    down = shift(add(d6, down), "tp", NTP, -1)
    up = shift(add(d1, up), "tp", NTP, 1)
    down = shift(add(d7, down), "tp", NTP, -1)
    return d0, up, down


def slots_kernel(chosen, own, up, down, out_ref):
    total = own[...].astype(f32) + up[...].astype(f32) + down[...].astype(f32)
    total = total.astype(bf16)
    out_ref[...] = jnp.zeros_like(out_ref)
    for k in range(SLOTS):
        out_ref[chosen[k]] = total[k * PIECE : (k + 1) * PIECE, :]


def to_slots(chosen, own, up, down):
    return pl.pallas_call(
        slots_kernel,
        in_specs=[smem(), vmem(), vmem(), vmem()],
        out_specs=vmem(),
        out_shape=jax.ShapeDtypeStruct((NCTX, PIECE, WIDTH), bf16),
        compiler_params=params(8),
        cost_estimate=cost(1e6, 2e6),
    )(chosen, own, up, down)


def collect_kernel(ids, got_ref, out_ref):
    out_ref[...] = jnp.zeros_like(out_ref)
    for s in range(NCTX):
        out_ref[ids[s]] += got_ref[s].astype(f32)


def collect(ids, got, blocks):
    return pl.pallas_call(
        collect_kernel,
        in_specs=[smem(), vmem()],
        out_specs=vmem(),
        out_shape=jax.ShapeDtypeStruct((blocks, PIECE, WIDTH), f32),
        compiler_params=params(8),
        cost_estimate=cost(1e6, 2e6),
    )(ids, got)


def shards(
    queries,
    latent_block_cache,
    selected_block_lists,
    output_gradient,
    output_weight,
    adapter_down,
    adapter_up,
    value_up_map,
    saved_head_input,
):
    ctx_axes = ("x", "y", "core")
    blocks_dev = latent_block_cache.shape[0]
    place = jnp.stack(
        [lax.axis_index("x"), lax.axis_index("y"), lax.axis_index("core"), lax.axis_index("tp")]
    ).astype(jnp.int32)

    holder = selected_block_lists // blocks_dev
    local = selected_block_lists - holder * blocks_dev
    every = jnp.arange(NCTX, dtype=jnp.int32)
    hit = holder[:, :, None] == every[None, None, :]
    wanted = jnp.max(jnp.where(hit, local[:, :, None], 0), axis=(0, 1))
    ids = lax.all_to_all(wanted, ctx_axes, split_axis=0, concat_axis=0, tiled=True)

    used = jnp.any(hit.reshape(GROUPS, GQ * hit.shape[1], NCTX), axis=1).astype(jnp.int32)
    rank = jnp.cumsum(used, axis=1)
    slot_hit = (used[:, None, :] == 1) & (
        rank[:, None, :] == jnp.arange(1, GSLOTS + 1, dtype=jnp.int32)[None, :, None]
    )
    chosen = jnp.sum(jnp.where(slot_hit, every[None, None, :], 0), axis=2).reshape(SLOTS)
    holder_groups = holder.reshape(GROUPS, GQ, holder.shape[1])
    picked = jnp.any(
        holder_groups[:, None, :, :] == chosen.reshape(GROUPS, GSLOTS)[:, :, None, None], axis=3
    )
    bias = jnp.where(picked, 0.0, MASKED).astype(f32)
    bias = jnp.concatenate([bias] * 4, axis=2)

    g_t = output_gradient.T
    mine, other, low, w_own = prep(place, g_t, adapter_up, output_weight.T, adapter_down)
    theirs = shift(other, "core", 2, 1)
    w_pair = shift(w_own, "core", 2, 1)

    cache_piece = turn_cache(place, jnp.swapaxes(latent_block_cache, 1, 2))
    rows = adapter_rows(saved_head_input, adapter_down)
    got = lax.all_to_all(
        serve(ids, cache_piece, low, rows), ctx_axes, split_axis=0, concat_axis=0, tiled=True
    )
    pieces = gather_tp(pick(chosen, got, g_t))
    down_part, up_gradient = adapter_grads(place, pieces, saved_head_input)
    down_gradient = lax.psum(down_part, ctx_axes).astype(f32)

    a_own, a_p1, a_m1, a_p2, a_m2, b_own, b_p1, b_m1, b_p2, b_m2 = head_partials(
        place, mine, theirs, w_own, w_pair
    )
    a_minus = shift(a_p1, "x", NX, 1)
    b_minus = shift(b_p1, "y", NY, 1)
    a_plus = shift(a_m1, "x", NX, -1)
    b_plus = shift(b_m1, "y", NY, -1)
    a_last_minus = shift(add(a_p2, a_minus[2:]), "x", NX, 1)
    a_last_plus = shift(add(a_m2, a_plus[:2]), "x", NX, -1)
    b_last_minus = shift(add(b_p2, b_minus[:2]), "y", NY, 1)
    b_last_plus = shift(add(b_m2, b_plus[2:]), "y", NY, -1)
    a_total = jnp.concatenate(
        [add(a_own[:2], a_plus[2:], a_last_minus), add(a_own[2:], a_minus[:2], a_last_plus)], axis=0
    )
    b_total = jnp.concatenate(
        [add(b_own[:2], b_plus[:2], b_last_minus), add(b_own[2:], b_minus[2:], b_last_plus)], axis=0
    )
    hg_a = reduce_second("y", a_total)
    hg_b = reduce_second("x", b_total)

    dq_t, *parts = attend(
        pieces, jnp.transpose(queries, (1, 2, 0)), hg_a, hg_b, value_up_map, bias
    )
    query_grads = jnp.transpose(dq_t, (2, 0, 1))

    own, up, down = reduce_tp(parts)
    returned = lax.all_to_all(
        to_slots(chosen, own, up, down), ctx_axes, split_axis=0, concat_axis=0, tiled=True
    )
    cache_grads = collect(ids, returned, blocks_dev)
    return (query_grads, cache_grads, down_gradient, up_gradient)


def solution(mesh):
    split = Mesh(mesh.devices.reshape(NX, NY, NCORE, NTP), ("x", "y", "core", "tp"))
    ctx = ("x", "y", "core")
    placed = (
        P(ctx, "tp", None),
        P(ctx, None, None),
        P(ctx, None),
        P(None, ctx),
        P("tp", ctx),
        P(None, "tp"),
        P(None, ctx),
        P("tp", None, None),
        P(ctx, "tp"),
    )
    return jax.shard_map(
        shards,
        mesh=split,
        in_specs=placed,
        out_specs=(P(ctx, "tp", None), P(ctx, "tp", None), P(None, "tp"), P(None, ctx)),
        check_vma=False,
    )
```

```python
import functools

import jax
import jax.numpy as jnp
from jax import lax
from jax.experimental import pallas as pl
from jax.experimental.pallas import tpu as pltpu
from jax.sharding import Mesh, PartitionSpec as P

SCORE_SCALE = 192.0 ** (-0.5)
ADAPTER_SCALE = 2.0
EXP2_SCALE = SCORE_SCALE * 1.4426950408889634

NX = 4
NY = 4
NCORE = 2
NCTX = 32
NTP = 8
GROUPS = 2
GSLOTS = 6
SLOTS = 12
BLOCK = 128
WIDTH = 576
LATENT = 512
VALUE = 128
HEADS_DEV = 16
QRY_DEV = 128
GQ = 64
RANK = 32
FEATS = 224
HEAD_IN = 2048
HALF_IN = 1024
CHIP_QRY = 256
PIECE = BLOCK // NTP
INFO_LANES = 640
SLOT_LANES = 768
DOWN_AT = 640
PREP_PAIRS = 4
HEAD_CUTS = 2
RING_COLS = 4
CORNER_FLOPS = 1e7
PICK_FLOPS = 1e11
SERVE_FLOPS = 1e6
GROUP_ROWS = GSLOTS * BLOCK
MASKED = -1e30

bf16 = jnp.bfloat16
f32 = jnp.float32

NN = (((1,), (0,)), ((), ()))
NT = (((1,), (1,)), ((), ()))
TN = (((0,), (0,)), ((), ()))


def mm(a, b, dims):
    return lax.dot_general(a, b, dims, preferred_element_type=f32)


def params(mib):
    return pltpu.CompilerParams(vmem_limit_bytes=mib * 1024 * 1024)


def cost(flops, nbytes):
    return pl.CostEstimate(flops=int(flops), bytes_accessed=int(nbytes), transcendentals=0)


def smem():
    return pl.BlockSpec(memory_space=pltpu.SMEM)


def vmem():
    return pl.BlockSpec(memory_space=pltpu.VMEM)


def prep_kernel(
    place,
    ids,
    g_ref,
    up_ref,
    w_ref,
    down_ref,
    saved_ref,
    cache_ref,
    rows_out,
    info,
    w_mine,
    w_other,
    cache_out,
    wcat,
    rows_t,
    block,
):
    step = pl.program_id(0)
    core = place[2]

    @pl.when(step == 0)
    def _():
        wcat[:FEATS, :] = w_ref[...]
        wcat[FEATS:, :] = (ADAPTER_SCALE * down_ref[...].astype(f32)).astype(bf16)
        w_mine[...] = wcat[:, pl.ds(pl.multiple_of(core * HALF_IN, HALF_IN), HALF_IN)]
        w_other[...] = wcat[:, pl.ds(pl.multiple_of((1 - core) * HALF_IN, HALF_IN), HALF_IN)]
        rows_t[...] = mm(down_ref[...], saved_ref[...], NT).astype(bf16)

    rows = rows_t[...]
    start = pl.multiple_of(place[3] * PIECE, PIECE)
    for pair in range(PREP_PAIRS):
        block[pair] = cache_ref[pair].T
        cache_out[pair] = block[pair, pl.ds(start, PIECE), :]
        g = g_ref[:, pair * 2 * QRY_DEV : (pair + 1) * 2 * QRY_DEV]
        low = mm(up_ref[...], g, NN).astype(bf16)
        rows_out[pair] = jnp.concatenate([g, low], axis=0).T
        for half in range(2):
            cols = slice(half * QRY_DEV, (half + 1) * QRY_DEV)
            at = 2 * pair + half
            info[at, :, 0:128] = low[:16, cols]
            info[at, :, 128:256] = low[16:, cols]
            info[at, :, 256:384] = rows[:16]
            info[at, :, 384:512] = rows[16:]
            number = ids[2 * PREP_PAIRS * step + at].astype(f32)
            info[at, :, 512:640] = jnp.full((16, 128), number, f32).astype(bf16)


def prep(place, ids, g_t, up, w_t, down, saved, cache_t):
    pairs = NX * NY
    blocks = cache_t.shape[0]
    step_blocks = blocks * PREP_PAIRS // pairs
    fixed = lambda s, p, i: (0, 0)
    moving = lambda s, p, i: (s, 0, 0)
    return pl.pallas_call(
        prep_kernel,
        grid_spec=pltpu.PrefetchScalarGridSpec(
            num_scalar_prefetch=2,
            grid=(pairs // PREP_PAIRS,),
            in_specs=[
                pl.BlockSpec((FEATS, PREP_PAIRS * 2 * QRY_DEV), lambda s, p, i: (0, s)),
                pl.BlockSpec((RANK, FEATS), fixed),
                pl.BlockSpec((FEATS, HEAD_IN), fixed),
                pl.BlockSpec((RANK, HEAD_IN), fixed),
                pl.BlockSpec((QRY_DEV, HEAD_IN), fixed),
                pl.BlockSpec((step_blocks, WIDTH, BLOCK), moving),
            ],
            out_specs=[
                pl.BlockSpec((PREP_PAIRS, 256, 256), moving),
                pl.BlockSpec((2 * PREP_PAIRS, 16, INFO_LANES), moving),
                pl.BlockSpec((256, HALF_IN), fixed),
                pl.BlockSpec((256, HALF_IN), fixed),
                pl.BlockSpec((step_blocks, PIECE, WIDTH), moving),
            ],
            scratch_shapes=[
                pltpu.VMEM((256, HEAD_IN), bf16),
                pltpu.VMEM((RANK, QRY_DEV), bf16),
                pltpu.VMEM((step_blocks, BLOCK, WIDTH), bf16),
            ],
        ),
        out_shape=[
            jax.ShapeDtypeStruct((pairs, 256, 256), bf16),
            jax.ShapeDtypeStruct((NCTX, 16, INFO_LANES), bf16),
            jax.ShapeDtypeStruct((256, HALF_IN), bf16),
            jax.ShapeDtypeStruct((256, HALF_IN), bf16),
            jax.ShapeDtypeStruct((blocks, PIECE, WIDTH), bf16),
        ],
        compiler_params=params(60),
        cost_estimate=cost(1e8, 6e6),
    )(place, ids, g_t, up, w_t, down, saved, cache_t)


def head_kernel(place, *refs):
    mine, theirs = refs[0:4], refs[4:8]
    w_own, w_pair = refs[8:10]
    (own, p1, m1, p2, m2, mark) = refs[10:]
    step = pl.program_id(0)
    rows = jnp.concatenate(
        [jnp.concatenate([m[0], t[0]], axis=1) for m, t in zip(mine, theirs)], axis=0
    )
    mark[...] = jnp.zeros_like(mark)
    steps = [
        [(own, 0), (own, 1), (own, 2), (own, 3)],
        [(p2, 0), (p2, 1), (p1, 0), (p1, 1)],
        [(p1, 0), (p1, 1), (m1, 0), (m1, 1)],
        [(m1, 0), (m1, 1), (m2, 0), (m2, 1)],
    ]
    for d1, places in enumerate(steps):

        @pl.when(step == d1)
        def _(places=places):
            for cut in range(HEAD_CUTS):
                size = HALF_IN // HEAD_CUTS
                cols = slice(cut * size, (cut + 1) * size)
                w = jnp.concatenate([w_own[:, cols], w_pair[:, cols]], axis=0)
                both = mm(rows, w, NN).astype(bf16)
                for d2, (ref, at) in enumerate(places):
                    ref[at, :, cols] = both[CHIP_QRY * d2 : CHIP_QRY * (d2 + 1)]


def head_partials(place, mine, theirs, w_own, w_pair):
    def row(d2):
        def index(s, p):
            on_x = jnp.where(p[2] == 0, s, d2)
            on_y = jnp.where(p[2] == 0, d2, s)
            return (lax.rem(p[0] + on_x, NX) * NY + lax.rem(p[1] + on_y, NY), 0, 0)

        return pl.BlockSpec((1, CHIP_QRY, 256), index)

    def whole():
        return pl.BlockSpec((256, HALF_IN), lambda s, p: (0, 0))

    def past(s, bound):
        return (s > bound).astype(jnp.int32)

    def out(count, block, index):
        return (
            pl.BlockSpec((block, CHIP_QRY, HALF_IN), lambda s, p: (index(s), 0, 0)),
            jax.ShapeDtypeStruct((count, CHIP_QRY, HALF_IN), bf16),
        )

    outs = [
        out(4, 4, lambda s: 0),
        out(4, 2, lambda s: past(s, 1)),
        out(4, 2, lambda s: past(s, 2)),
        out(2, 2, lambda s: 0),
        out(2, 2, lambda s: 0),
        (
            pl.BlockSpec((8, 128), lambda s, p: (0, 0)),
            jax.ShapeDtypeStruct((8, 128), f32),
        ),
    ]
    return pl.pallas_call(
        head_kernel,
        grid_spec=pltpu.PrefetchScalarGridSpec(
            num_scalar_prefetch=1,
            grid=(4,),
            in_specs=[row(i) for i in range(4)] * 2 + [whole(), whole()],
            out_specs=[o[0] for o in outs],
        ),
        out_shape=[o[1] for o in outs],
        compiler_params=params(60),
        cost_estimate=cost(4.3e9, 13e6),
    )(place, *[mine] * 4, *[theirs] * 4, w_own, w_pair)


def ring(value, order, by):
    pairs = []
    for x in range(NX):
        for y in range(NY):
            for core in range(NCORE):
                if core == order:
                    to = ((x + by) % NX, y)
                else:
                    to = (x, (y + by) % NY)
                pairs.append(((x * NY + y) * 2 + core, (to[0] * NY + to[1]) * 2 + core))
    return lax.ppermute(value, ("x", "y", "core"), pairs)


def shift(value, axis, size, by):
    return lax.ppermute(value, axis, [(i, (i + by) % size) for i in range(size)])


def add(*terms):
    total = terms[0].astype(f32)
    for t in terms[1:]:
        total = total + t.astype(f32)
    return total.astype(bf16)


def call_whole(kernel, outs, mib, flops, nbytes, *args):
    return pl.pallas_call(
        kernel,
        in_specs=[vmem()] * len(args),
        out_specs=[vmem()] * len(outs),
        out_shape=[jax.ShapeDtypeStruct(o, bf16) for o in outs],
        compiler_params=params(mib),
        cost_estimate=cost(flops, nbytes),
    )(*args)


def relay_kernel(p, m, minus, plus, mark, o1, o2):
    o1[...] = add(p[...], minus[...])
    o2[...] = add(m[...], plus[...])


def columns(count, rest, at=0):
    block = (count,) + rest + (HALF_IN // RING_COLS,)
    if rest:
        return pl.BlockSpec(block, lambda s: (at, 0, s))
    return pl.BlockSpec(block, lambda s: (0, s))


def relay(*args):
    return pl.pallas_call(
        relay_kernel,
        grid=(RING_COLS,),
        in_specs=[columns(2, (CHIP_QRY,), at) for at in (0, 0, 1, 0)]
        + [pl.BlockSpec((16, 128), lambda s: (0, 0))],
        out_specs=[columns(2, (CHIP_QRY,))] * 2,
        out_shape=[jax.ShapeDtypeStruct((2, CHIP_QRY, HALF_IN), bf16)] * 2,
        compiler_params=params(60),
        cost_estimate=cost(1e7, 6e6),
    )(*args)


def corner_kernel(own, minus, plus, last_minus, last_plus, mark_a, mark_b, *outs):
    for i in range(2):
        outs[i][...] = add(own[i], plus[i], last_minus[i])
        outs[2 + i][...] = add(own[2 + i], minus[i], last_plus[i])


def corner(*args):
    two = columns(2, (CHIP_QRY,))
    return pl.pallas_call(
        corner_kernel,
        grid=(RING_COLS,),
        in_specs=[columns(4, (CHIP_QRY,)), two, columns(2, (CHIP_QRY,), 1), two, two]
        + [pl.BlockSpec((16, 128), lambda s: (0, 0))] * 2,
        out_specs=[columns(CHIP_QRY, ())] * 4,
        out_shape=[jax.ShapeDtypeStruct((CHIP_QRY, HALF_IN), bf16)] * 4,
        compiler_params=params(60),
        cost_estimate=cost(1e7, 8e6),
    )(*args)


def total_kernel(place, a, b, c, d, mine, other):
    core = place[2]
    here = pl.ds(pl.multiple_of(core * QRY_DEV, QRY_DEV), QRY_DEV)
    there = pl.ds(pl.multiple_of((1 - core) * QRY_DEV, QRY_DEV), QRY_DEV)
    mine[...] = add(a[here, :], b[here, :], c[here, :], d[here, :])
    other[...] = add(a[there, :], b[there, :], c[there, :], d[there, :])


def total(place, *args):
    return pl.pallas_call(
        total_kernel,
        in_specs=[smem()] + [vmem()] * 4,
        out_specs=[vmem()] * 2,
        out_shape=[jax.ShapeDtypeStruct((QRY_DEV, HALF_IN), bf16)] * 2,
        compiler_params=params(60),
        cost_estimate=cost(1e6, 3e6),
    )(place, *args)


def pick_kernel(chosen, got, up_ref, piece, down_out):
    for k in range(SLOTS):
        piece[k * PIECE : (k + 1) * PIECE, :] = got[chosen[k], :, :WIDTH]
    base = SLOTS * PIECE
    piece[base : base + 16, :] = jnp.zeros((16, WIDTH), bf16)
    piece[base : base + 16, :FEATS] = up_ref[:16]
    piece[base : base + 16, 256 : 256 + FEATS] = up_ref[16:]
    down = got[0, :, DOWN_AT:].astype(f32)
    for s in range(1, NCTX):
        down = down + got[s, :, DOWN_AT:].astype(f32)
    down_out[...] = down.astype(bf16)


def pick(chosen, got, up):
    outs = [(SLOTS * PIECE + 16, WIDTH), (16, 128)]
    return pl.pallas_call(
        pick_kernel,
        in_specs=[smem(), vmem(), vmem()],
        out_specs=[vmem()] * 2,
        out_shape=[jax.ShapeDtypeStruct(o, bf16) for o in outs],
        compiler_params=params(60),
        cost_estimate=cost(PICK_FLOPS, 1e6),
    )(chosen, got, up)


def serve_kernel(ids, cache_ref, info, saved_ref, mark, out_ref):
    low0 = info[0, :, 0:128].astype(f32)
    low1 = info[0, :, 128:256].astype(f32)
    for s in range(1, NCTX):
        low0 = low0 + info[s, :, 0:128].astype(f32)
        low1 = low1 + info[s, :, 128:256].astype(f32)
    low = (ADAPTER_SCALE * jnp.concatenate([low0, low1], axis=0)).astype(bf16)
    down = mm(low, saved_ref[...], NN).astype(bf16)
    for s in range(NCTX):
        row, col = 16 * (s // 16), 128 * (s % 16)
        out_ref[s, :, :WIDTH] = cache_ref[ids[s]]
        out_ref[s, :, DOWN_AT:] = down[row : row + 16, col : col + 128]


def serve(ids, cache_piece, info, saved, mark):
    return pl.pallas_call(
        serve_kernel,
        in_specs=[smem()] + [vmem()] * 4,
        out_specs=vmem(),
        out_shape=jax.ShapeDtypeStruct((NCTX, PIECE, SLOT_LANES), bf16),
        compiler_params=params(60),
        cost_estimate=cost(SERVE_FLOPS, 2e6),
    )(ids, cache_piece, info, saved, mark)


def up_kernel(info, g_ref, mark, up_out, rows_all):
    for s in range(NCTX):
        rows_all[0:16, s * 128 : (s + 1) * 128] = info[s, :, 256:384]
        rows_all[16:32, s * 128 : (s + 1) * 128] = info[s, :, 384:512]
    up_out[...] = mm(rows_all[...], g_ref[...], NT).astype(bf16)


def up_partial(info, g_t, mark):
    return pl.pallas_call(
        up_kernel,
        in_specs=[vmem()] * 3,
        out_specs=vmem(),
        out_shape=jax.ShapeDtypeStruct((RANK, FEATS), bf16),
        scratch_shapes=[pltpu.VMEM((RANK, NCTX * QRY_DEV), bf16)],
        compiler_params=params(60),
        cost_estimate=cost(1e8, 3e6),
    )(info, g_t, mark)


def gather_tp(own):
    pieces = [None] * NTP
    pieces[0] = own
    forward = own
    back = own
    for step in range(1, 5):
        forward = shift(forward, "tp", NTP, -1)
        pieces[step] = forward
        if step < 4:
            back = shift(back, "tp", NTP, 1)
            pieces[NTP - step] = back
    return pieces


def attend_kernel(place, *refs):
    pieces = refs[:NTP]
    q_ref, vu_ref, bias_ref, hg_mine, hg_other = refs[NTP : NTP + 5]
    dq_ref, up_ref = refs[NTP + 5 : NTP + 7]
    outs = refs[NTP + 7 : NTP + 16]
    keys, keys_t, spread, ds_all, p_all, q_all, og_all = refs[NTP + 16 :]
    step = pl.program_id(0)
    span = GSLOTS * PIECE
    lanes = 4 * GQ

    @pl.when(step == 0)
    def _():
        for d in range(NTP):
            for g in range(GROUPS):
                keys[g, d * span : (d + 1) * span, :] = pieces[d][g * span : (g + 1) * span, :]
        for g in range(GROUPS):
            keys_t[g] = keys[g].T
        spread[...] = jnp.zeros_like(spread)
        base = SLOTS * PIECE
        total = pieces[0][base : base + 16, :512].astype(f32)
        for d in range(1, NTP):
            total = total + pieces[d][base : base + 16, :512].astype(f32)
        up_ref[:16, :] = ADAPTER_SCALE * total[:, :FEATS]
        up_ref[16:, :] = ADAPTER_SCALE * total[:, 256 : 256 + FEATS]

    here = pl.ds(pl.multiple_of(step * lanes, lanes), lanes)
    hg = jnp.where(step // 2 == place[2], hg_mine[...], hg_other[...])
    maps = jnp.concatenate([vu_ref[h] for h in range(4)], axis=1)
    dqs = []
    for g in range(GROUPS):
        q4 = jnp.concatenate([q_ref[h][:, g * GQ : (g + 1) * GQ] for h in range(4)], axis=1)
        for h in range(4):
            cols = slice(h * VALUE, (h + 1) * VALUE)
            spread[g, h * GQ : (h + 1) * GQ, cols] = hg[g * GQ : (g + 1) * GQ, cols]
        og = mm(maps, spread[g], NT).astype(bf16)
        q_all[g, :, here] = q4
        og_all[g, :, here] = og
        s = mm(keys[g], q4, NN)
        s = s.reshape(NTP, GSLOTS, PIECE, lanes) * EXP2_SCALE + bias_ref[g][None, :, None, :]
        s = s.reshape(GROUP_ROWS, lanes)
        e = jnp.exp2(s - jnp.max(s, axis=0, keepdims=True))
        share = 1.0 / jnp.sum(e, axis=0, keepdims=True)
        dp = mm(keys[g, :, :LATENT], og, NN)
        delta = jnp.sum(e * dp, axis=0, keepdims=True) * share
        ds = (e * ((dp - delta) * (share * SCORE_SCALE))).astype(bf16)
        p_all[g, :, here] = (e * share).astype(bf16)
        ds_all[g, :, here] = ds
        dqs.append(mm(keys_t[g], ds, NN).astype(bf16))
    for h in range(4):
        cols = slice(h * GQ, (h + 1) * GQ)
        dq_ref[h] = jnp.concatenate([dqs[0][:, cols], dqs[1][:, cols]], axis=1)

    @pl.when(step == pl.num_programs(0) - 1)
    def _():
        for g in range(GROUPS):
            grads = mm(ds_all[g], q_all[g], NT)
            latent = grads[:, :LATENT] + mm(p_all[g], og_all[g], NT)
            latent = latent.astype(bf16)
            rope = grads[:, LATENT:].astype(bf16)
            for d in range(NTP):
                ref = outs[d] if d < 4 else (outs[4 + g] if d == 4 else outs[d + 1])
                at = 0 if d == 4 else g * span
                ref[at : at + span, :LATENT] = latent[d * span : (d + 1) * span]
                ref[at : at + span, LATENT:] = rope[d * span : (d + 1) * span]


def attend(place, pieces, q_t, vu, bias, hg_mine, hg_other):
    span = GSLOTS * PIECE
    whole = lambda s: (0, 0)
    rows = [2 * span] * 4 + [span] * 2 + [2 * span] * 3
    out_specs = [
        pl.BlockSpec((4, WIDTH, QRY_DEV), lambda s: (s, 0, 0)),
        pl.BlockSpec((RANK, FEATS), whole),
    ]
    out_specs += [pl.BlockSpec((n, WIDTH), whole) for n in rows]
    out_shape = [
        jax.ShapeDtypeStruct((HEADS_DEV, WIDTH, QRY_DEV), bf16),
        jax.ShapeDtypeStruct((RANK, FEATS), f32),
    ]
    out_shape += [jax.ShapeDtypeStruct((n, WIDTH), bf16) for n in rows]
    hg_spec = pl.BlockSpec((QRY_DEV, 4 * VALUE), lambda s: (0, lax.rem(s, 2)))
    width = HEADS_DEV * GQ
    return pl.pallas_call(
        attend_kernel,
        grid=(HEADS_DEV // 4,),
        in_specs=[smem()]
        + [pl.BlockSpec(pieces[0].shape, whole)] * NTP
        + [
            pl.BlockSpec((4, WIDTH, QRY_DEV), lambda s: (s, 0, 0)),
            pl.BlockSpec((4, LATENT, VALUE), lambda s: (s, 0, 0)),
            pl.BlockSpec(bias.shape, lambda s: (0, 0, 0)),
        ]
        + [hg_spec] * 2,
        out_specs=out_specs,
        out_shape=out_shape,
        scratch_shapes=[
            pltpu.VMEM((GROUPS, GROUP_ROWS, WIDTH), bf16),
            pltpu.VMEM((GROUPS, WIDTH, GROUP_ROWS), bf16),
            pltpu.VMEM((GROUPS, 4 * GQ, 4 * VALUE), bf16),
            pltpu.VMEM((GROUPS, GROUP_ROWS, width), bf16),
            pltpu.VMEM((GROUPS, GROUP_ROWS, width), bf16),
            pltpu.VMEM((GROUPS, WIDTH, width), bf16),
            pltpu.VMEM((GROUPS, LATENT, width), bf16),
        ],
        compiler_params=params(60),
        cost_estimate=cost(1e10, 1.2e7),
    )(place, *pieces, q_t, vu, bias, hg_mine, hg_other)


def reduce_tp(parts):
    d0, d1, d2, d3, d4a, d4b, d5, d6, d7 = parts
    half = d4a.shape[0]
    up = shift(d4a, "tp", NTP, 1)
    down = shift(d4b, "tp", NTP, -1)
    up = shift(jnp.concatenate([add(d3[:half], up), d3[half:]], axis=0), "tp", NTP, 1)
    down = shift(jnp.concatenate([d5[:half], add(d5[half:], down)], axis=0), "tp", NTP, -1)
    up = shift(add(d2, up), "tp", NTP, 1)
    down = shift(add(d6, down), "tp", NTP, -1)
    up = shift(add(d1, up), "tp", NTP, 1)
    down = shift(add(d7, down), "tp", NTP, -1)
    return d0, up, down


def slots_kernel(chosen, own, up, down, sums, out_ref):
    total = own[...].astype(f32) + up[...].astype(f32) + down[...].astype(f32)
    total = total.astype(bf16)
    empty = jnp.zeros((PIECE, WIDTH), bf16)
    for s in range(NCTX):
        out_ref[s, :, :WIDTH] = empty
        out_ref[s, :, DOWN_AT:] = sums[...]
    for k in range(SLOTS):
        out_ref[chosen[k], :, :WIDTH] = total[k * PIECE : (k + 1) * PIECE, :]


def to_slots(chosen, own, up, down, sums):
    return pl.pallas_call(
        slots_kernel,
        in_specs=[smem()] + [vmem()] * 4,
        out_specs=vmem(),
        out_shape=jax.ShapeDtypeStruct((NCTX, PIECE, SLOT_LANES), bf16),
        compiler_params=params(60),
        cost_estimate=cost(1e6, 2e6),
    )(chosen, own, up, down, sums)


def collect_kernel(ids, got_ref, out_ref, down_ref):
    out_ref[...] = jnp.zeros_like(out_ref)
    for s in range(NCTX):
        row, col = 16 * (s // 16), 128 * (s % 16)
        down_ref[row : row + 16, col : col + 128] = got_ref[s, :, DOWN_AT:].astype(f32)
        out_ref[ids[s]] += got_ref[s, :, :WIDTH].astype(f32)


def collect(ids, got, blocks):
    return pl.pallas_call(
        collect_kernel,
        in_specs=[smem(), vmem()],
        out_specs=[vmem(), vmem()],
        out_shape=[
            jax.ShapeDtypeStruct((blocks, PIECE, WIDTH), f32),
            jax.ShapeDtypeStruct((RANK, HEAD_IN), f32),
        ],
        compiler_params=params(60),
        cost_estimate=cost(1e6, 2e6),
    )(ids, got)


def shards(
    queries,
    latent_block_cache,
    selected_block_lists,
    output_gradient,
    output_weight,
    adapter_down,
    adapter_up,
    value_up_map,
    saved_head_input,
):
    ctx_axes = ("x", "y", "core")
    blocks_dev = latent_block_cache.shape[0]
    place = jnp.stack(
        [lax.axis_index("x"), lax.axis_index("y"), lax.axis_index("core"), lax.axis_index("tp")]
    ).astype(jnp.int32)

    holder = selected_block_lists // blocks_dev
    local = selected_block_lists - holder * blocks_dev
    every = jnp.arange(NCTX, dtype=jnp.int32)
    hit = holder[:, :, None] == every[None, None, :]
    wanted = jnp.max(jnp.where(hit, local[:, :, None], 0), axis=(0, 1))
    g_t = output_gradient.T
    mine, info, w_own, w_other, cache_piece = prep(
        place,
        wanted,
        g_t,
        adapter_up,
        output_weight.T,
        adapter_down,
        saved_head_input,
        jnp.swapaxes(latent_block_cache, 1, 2),
    )
    theirs = shift(mine, "core", 2, 1)
    w_pair = shift(w_other, "core", 2, 1)
    info = lax.all_to_all(info, ctx_axes, split_axis=0, concat_axis=0, tiled=True)

    used = jnp.any(hit.reshape(GROUPS, GQ * hit.shape[1], NCTX), axis=1).astype(jnp.int32)
    rank = jnp.cumsum(used, axis=1)
    slot_hit = (used[:, None, :] == 1) & (
        rank[:, None, :] == jnp.arange(1, GSLOTS + 1, dtype=jnp.int32)[None, :, None]
    )
    chosen = jnp.sum(jnp.where(slot_hit, every[None, None, :], 0), axis=2).reshape(SLOTS)
    holder_groups = holder.reshape(GROUPS, GQ, holder.shape[1])
    picked = jnp.any(
        holder_groups[:, None, :, :] == chosen.reshape(GROUPS, GSLOTS)[:, :, None, None], axis=3
    )
    bias = jnp.where(picked, 0.0, MASKED).astype(f32)
    bias = jnp.concatenate([bias] * 4, axis=2)

    own, p1, m1, p2, m2, mark = head_partials(place, mine, theirs, w_own, w_pair)
    ids = (info[:, 0, 512].astype(f32) + mark[0, 0]).astype(jnp.int32)
    minus = ring(p1, 0, 1)
    plus = ring(m1, 0, -1)

    slots = serve(ids, cache_piece, info, saved_head_input, mark)
    got = lax.all_to_all(slots, ctx_axes, split_axis=0, concat_axis=0, tiled=True)
    up_part = up_partial(info, g_t, mark)
    piece, down_sums = pick(chosen, got, up_part)
    pieces = gather_tp(piece)
    p2, m2 = relay(p2, m2, minus, plus, pieces[1])
    last_minus = ring(p2, 0, 1)
    last_plus = ring(m2, 0, -1)
    sums = corner(own, minus, plus, last_minus, last_plus, pieces[3], pieces[6])
    hg_mine, hg_other = total(place, sums[0], *[ring(sums[i], 1, i) for i in (1, 2, 3)])
    hg_other = shift(hg_other, "core", 2, 1)

    dq_t, up_gradient, *parts = attend(
        place,
        pieces,
        jnp.transpose(queries, (1, 2, 0)),
        value_up_map,
        bias,
        hg_mine,
        hg_other,
    )
    query_grads = jnp.transpose(dq_t, (2, 0, 1))

    own, up, down = reduce_tp(parts)
    slots = to_slots(chosen, own, up, down, down_sums)
    returned = lax.all_to_all(slots, ctx_axes, split_axis=0, concat_axis=0, tiled=True)
    cache_grads, down_gradient = collect(ids, returned, blocks_dev)
    return (query_grads, cache_grads, down_gradient, up_gradient)


def solution(mesh):
    split = Mesh(mesh.devices.reshape(NX, NY, NCORE, NTP), ("x", "y", "core", "tp"))
    ctx = ("x", "y", "core")
    placed = (
        P(ctx, "tp", None),
        P(ctx, None, None),
        P(ctx, None),
        P(None, ctx),
        P("tp", ctx),
        P(None, "tp"),
        P(None, ctx),
        P("tp", None, None),
        P(ctx, "tp"),
    )
    return jax.shard_map(
        shards,
        mesh=split,
        in_specs=placed,
        out_specs=(P(ctx, "tp", None), P(ctx, "tp", None), P(None, "tp"), P(None, ctx)),
        check_vma=False,
    )
```

```python
import functools

import jax
import jax.numpy as jnp
from jax import lax
from jax.experimental import pallas as pl
from jax.experimental.pallas import tpu as pltpu
from jax.sharding import Mesh, PartitionSpec as P

SCORE_SCALE = 192.0 ** (-0.5)
ADAPTER_SCALE = 2.0
EXP2_SCALE = SCORE_SCALE * 1.4426950408889634

NX = 4
NY = 4
NCORE = 2
NCTX = 32
NTP = 8
GROUPS = 2
GSLOTS = 6
SLOTS = 12
BLOCK = 128
WIDTH = 576
LATENT = 512
VALUE = 128
HEADS_DEV = 16
QRY_DEV = 128
GQ = 64
RANK = 32
FEATS = 224
HEAD_IN = 2048
HALF_IN = 1024
CHIP_QRY = 256
PIECE = BLOCK // NTP
INFO_LANES = 640
SLOT_LANES = 768
DOWN_AT = 640
PREP_PAIRS = 8
QUADS = 4
ATTEND_MIB = 40
HEAD_CUTS = 2
RING_COLS = 2
CORNER_FLOPS = 1e7
PICK_FLOPS = 1e11
SERVE_FLOPS = 1e6
GROUP_ROWS = GSLOTS * BLOCK
MASKED = -1e30

bf16 = jnp.bfloat16
f32 = jnp.float32

NN = (((1,), (0,)), ((), ()))
NT = (((1,), (1,)), ((), ()))
TN = (((0,), (0,)), ((), ()))


def mm(a, b, dims):
    return lax.dot_general(a, b, dims, preferred_element_type=f32)


def params(mib):
    return pltpu.CompilerParams(vmem_limit_bytes=mib * 1024 * 1024)


def cost(flops, nbytes):
    return pl.CostEstimate(flops=int(flops), bytes_accessed=int(nbytes), transcendentals=0)


def smem():
    return pl.BlockSpec(memory_space=pltpu.SMEM)


def vmem():
    return pl.BlockSpec(memory_space=pltpu.VMEM)


def prep_kernel(
    place,
    ids,
    g_ref,
    up_ref,
    w_ref,
    down_ref,
    saved_ref,
    cache_ref,
    rows_out,
    info,
    w_mine,
    w_other,
    cache_out,
    wcat,
    rows_t,
    block,
):
    step = pl.program_id(0)
    core = place[2]

    @pl.when(step == 0)
    def _():
        wcat[:FEATS, :] = w_ref[...]
        wcat[FEATS:, :] = (ADAPTER_SCALE * down_ref[...].astype(f32)).astype(bf16)
        w_mine[...] = wcat[:, pl.ds(pl.multiple_of(core * HALF_IN, HALF_IN), HALF_IN)]
        w_other[...] = wcat[:, pl.ds(pl.multiple_of((1 - core) * HALF_IN, HALF_IN), HALF_IN)]
        rows_t[...] = mm(down_ref[...], saved_ref[...], NT).astype(bf16)

    rows = rows_t[...]
    start = pl.multiple_of(place[3] * PIECE, PIECE)
    for pair in range(PREP_PAIRS):
        block[pair] = cache_ref[pair].T
        cache_out[pair] = block[pair, pl.ds(start, PIECE), :]
        g = g_ref[:, pair * 2 * QRY_DEV : (pair + 1) * 2 * QRY_DEV]
        low = mm(up_ref[...], g, NN).astype(bf16)
        rows_out[pair] = jnp.concatenate([g, low], axis=0).T
        for half in range(2):
            cols = slice(half * QRY_DEV, (half + 1) * QRY_DEV)
            at = 2 * pair + half
            info[at, :, 0:128] = low[:16, cols]
            info[at, :, 128:256] = low[16:, cols]
            info[at, :, 256:384] = rows[:16]
            info[at, :, 384:512] = rows[16:]
            number = ids[2 * PREP_PAIRS * step + at].astype(f32)
            info[at, :, 512:640] = jnp.full((16, 128), number, f32).astype(bf16)


def prep(place, ids, g_t, up, w_t, down, saved, cache_t):
    pairs = NX * NY
    blocks = cache_t.shape[0]
    step_blocks = blocks * PREP_PAIRS // pairs
    fixed = lambda s, p, i: (0, 0)
    moving = lambda s, p, i: (s, 0, 0)
    return pl.pallas_call(
        prep_kernel,
        grid_spec=pltpu.PrefetchScalarGridSpec(
            num_scalar_prefetch=2,
            grid=(pairs // PREP_PAIRS,),
            in_specs=[
                pl.BlockSpec((FEATS, PREP_PAIRS * 2 * QRY_DEV), lambda s, p, i: (0, s)),
                pl.BlockSpec((RANK, FEATS), fixed),
                pl.BlockSpec((FEATS, HEAD_IN), fixed),
                pl.BlockSpec((RANK, HEAD_IN), fixed),
                pl.BlockSpec((QRY_DEV, HEAD_IN), fixed),
                pl.BlockSpec((step_blocks, WIDTH, BLOCK), moving),
            ],
            out_specs=[
                pl.BlockSpec((PREP_PAIRS, 256, 256), moving),
                pl.BlockSpec((2 * PREP_PAIRS, 16, INFO_LANES), moving),
                pl.BlockSpec((256, HALF_IN), fixed),
                pl.BlockSpec((256, HALF_IN), fixed),
                pl.BlockSpec((step_blocks, PIECE, WIDTH), moving),
            ],
            scratch_shapes=[
                pltpu.VMEM((256, HEAD_IN), bf16),
                pltpu.VMEM((RANK, QRY_DEV), bf16),
                pltpu.VMEM((step_blocks, BLOCK, WIDTH), bf16),
            ],
        ),
        out_shape=[
            jax.ShapeDtypeStruct((pairs, 256, 256), bf16),
            jax.ShapeDtypeStruct((NCTX, 16, INFO_LANES), bf16),
            jax.ShapeDtypeStruct((256, HALF_IN), bf16),
            jax.ShapeDtypeStruct((256, HALF_IN), bf16),
            jax.ShapeDtypeStruct((blocks, PIECE, WIDTH), bf16),
        ],
        compiler_params=params(60),
        cost_estimate=cost(1e8, 6e6),
    )(place, ids, g_t, up, w_t, down, saved, cache_t)


def head_kernel(place, *refs):
    mine, theirs = refs[0:4], refs[4:8]
    w_own, w_pair = refs[8:10]
    (own, p1, m1, p2, m2, mark) = refs[10:]
    step = pl.program_id(0)
    rows = jnp.concatenate(
        [jnp.concatenate([m[0], t[0]], axis=1) for m, t in zip(mine, theirs)], axis=0
    )
    mark[...] = jnp.zeros_like(mark)
    steps = [
        [(own, 0), (own, 1), (own, 2), (own, 3)],
        [(p2, 0), (p2, 1), (p1, 0), (p1, 1)],
        [(p1, 0), (p1, 1), (m1, 0), (m1, 1)],
        [(m1, 0), (m1, 1), (m2, 0), (m2, 1)],
    ]
    for d1, places in enumerate(steps):

        @pl.when(step == d1)
        def _(places=places):
            for cut in range(HEAD_CUTS):
                size = HALF_IN // HEAD_CUTS
                cols = slice(cut * size, (cut + 1) * size)
                w = jnp.concatenate([w_own[:, cols], w_pair[:, cols]], axis=0)
                both = mm(rows, w, NN).astype(bf16)
                for d2, (ref, at) in enumerate(places):
                    ref[at, :, cols] = both[CHIP_QRY * d2 : CHIP_QRY * (d2 + 1)]


def head_partials(place, mine, theirs, w_own, w_pair):
    def row(d2):
        def index(s, p):
            on_x = jnp.where(p[2] == 0, s, d2)
            on_y = jnp.where(p[2] == 0, d2, s)
            return (lax.rem(p[0] + on_x, NX) * NY + lax.rem(p[1] + on_y, NY), 0, 0)

        return pl.BlockSpec((1, CHIP_QRY, 256), index)

    def whole():
        return pl.BlockSpec((256, HALF_IN), lambda s, p: (0, 0))

    def past(s, bound):
        return (s > bound).astype(jnp.int32)

    def out(count, block, index):
        return (
            pl.BlockSpec((block, CHIP_QRY, HALF_IN), lambda s, p: (index(s), 0, 0)),
            jax.ShapeDtypeStruct((count, CHIP_QRY, HALF_IN), bf16),
        )

    outs = [
        out(4, 4, lambda s: 0),
        out(4, 2, lambda s: past(s, 1)),
        out(4, 2, lambda s: past(s, 2)),
        out(2, 2, lambda s: 0),
        out(2, 2, lambda s: 0),
        (
            pl.BlockSpec((8, 128), lambda s, p: (0, 0)),
            jax.ShapeDtypeStruct((8, 128), f32),
        ),
    ]
    return pl.pallas_call(
        head_kernel,
        grid_spec=pltpu.PrefetchScalarGridSpec(
            num_scalar_prefetch=1,
            grid=(4,),
            in_specs=[row(i) for i in range(4)] * 2 + [whole(), whole()],
            out_specs=[o[0] for o in outs],
        ),
        out_shape=[o[1] for o in outs],
        compiler_params=params(60),
        cost_estimate=cost(4.3e9, 13e6),
    )(place, *[mine] * 4, *[theirs] * 4, w_own, w_pair)


def ring(value, order, by):
    pairs = []
    for x in range(NX):
        for y in range(NY):
            for core in range(NCORE):
                if core == order:
                    to = ((x + by) % NX, y)
                else:
                    to = (x, (y + by) % NY)
                pairs.append(((x * NY + y) * 2 + core, (to[0] * NY + to[1]) * 2 + core))
    return lax.ppermute(value, ("x", "y", "core"), pairs)


def shift(value, axis, size, by):
    return lax.ppermute(value, axis, [(i, (i + by) % size) for i in range(size)])


def add(*terms):
    total = terms[0].astype(f32)
    for t in terms[1:]:
        total = total + t.astype(f32)
    return total.astype(bf16)


def call_whole(kernel, outs, mib, flops, nbytes, *args):
    return pl.pallas_call(
        kernel,
        in_specs=[vmem()] * len(args),
        out_specs=[vmem()] * len(outs),
        out_shape=[jax.ShapeDtypeStruct(o, bf16) for o in outs],
        compiler_params=params(mib),
        cost_estimate=cost(flops, nbytes),
    )(*args)


def relay_kernel(p, m, minus, plus, mark, o1, o2):
    o1[...] = add(p[...], minus[...])
    o2[...] = add(m[...], plus[...])


def columns(count, rest, at=0):
    block = (count,) + rest + (HALF_IN // RING_COLS,)
    if rest:
        return pl.BlockSpec(block, lambda s: (at, 0, s))
    return pl.BlockSpec(block, lambda s: (0, s))


def relay(*args):
    return pl.pallas_call(
        relay_kernel,
        grid=(RING_COLS,),
        in_specs=[columns(2, (CHIP_QRY,), at) for at in (0, 0, 1, 0)]
        + [pl.BlockSpec((16, 128), lambda s: (0, 0))],
        out_specs=[columns(2, (CHIP_QRY,))] * 2,
        out_shape=[jax.ShapeDtypeStruct((2, CHIP_QRY, HALF_IN), bf16)] * 2,
        compiler_params=params(36),
        cost_estimate=cost(1e7, 6e6),
    )(*args)


def corner_kernel(own, minus, plus, last_minus, last_plus, mark_a, mark_b, *outs):
    for i in range(2):
        outs[i][...] = add(own[i], plus[i], last_minus[i])
        outs[2 + i][...] = add(own[2 + i], minus[i], last_plus[i])


def corner(*args):
    two = columns(2, (CHIP_QRY,))
    return pl.pallas_call(
        corner_kernel,
        grid=(RING_COLS,),
        in_specs=[columns(4, (CHIP_QRY,)), two, columns(2, (CHIP_QRY,), 1), two, two]
        + [pl.BlockSpec((16, 128), lambda s: (0, 0))] * 2,
        out_specs=[columns(CHIP_QRY, ())] * 4,
        out_shape=[jax.ShapeDtypeStruct((CHIP_QRY, HALF_IN), bf16)] * 4,
        compiler_params=params(36),
        cost_estimate=cost(1e7, 8e6),
    )(*args)


def total_kernel(place, a, b, c, d, mine, other):
    core = place[2]
    here = pl.ds(pl.multiple_of(core * QRY_DEV, QRY_DEV), QRY_DEV)
    there = pl.ds(pl.multiple_of((1 - core) * QRY_DEV, QRY_DEV), QRY_DEV)
    mine[...] = add(a[here, :], b[here, :], c[here, :], d[here, :])
    other[...] = add(a[there, :], b[there, :], c[there, :], d[there, :])


def total(place, *args):
    return pl.pallas_call(
        total_kernel,
        in_specs=[smem()] + [vmem()] * 4,
        out_specs=[vmem()] * 2,
        out_shape=[jax.ShapeDtypeStruct((QRY_DEV, HALF_IN), bf16)] * 2,
        compiler_params=params(36),
        cost_estimate=cost(1e6, 3e6),
    )(place, *args)


def pick_kernel(chosen, got, up_ref, piece, down_out):
    for k in range(SLOTS):
        piece[k * PIECE : (k + 1) * PIECE, :] = got[chosen[k], :, :WIDTH]
    base = SLOTS * PIECE
    piece[base : base + 16, :] = jnp.zeros((16, WIDTH), bf16)
    piece[base : base + 16, :FEATS] = up_ref[:16]
    piece[base : base + 16, 256 : 256 + FEATS] = up_ref[16:]
    down = got[0, :, DOWN_AT:].astype(f32)
    for s in range(1, NCTX):
        down = down + got[s, :, DOWN_AT:].astype(f32)
    down_out[...] = down.astype(bf16)


def pick(chosen, got, up):
    outs = [(SLOTS * PIECE + 16, WIDTH), (16, 128)]
    return pl.pallas_call(
        pick_kernel,
        in_specs=[smem(), vmem(), vmem()],
        out_specs=[vmem()] * 2,
        out_shape=[jax.ShapeDtypeStruct(o, bf16) for o in outs],
        compiler_params=params(36),
        cost_estimate=cost(PICK_FLOPS, 1e6),
    )(chosen, got, up)


def serve_kernel(ids, cache_ref, info, saved_ref, mark, out_ref):
    low0 = info[0, :, 0:128].astype(f32)
    low1 = info[0, :, 128:256].astype(f32)
    for s in range(1, NCTX):
        low0 = low0 + info[s, :, 0:128].astype(f32)
        low1 = low1 + info[s, :, 128:256].astype(f32)
    low = (ADAPTER_SCALE * jnp.concatenate([low0, low1], axis=0)).astype(bf16)
    down = mm(low, saved_ref[...], NN).astype(bf16)
    for s in range(NCTX):
        row, col = 16 * (s // 16), 128 * (s % 16)
        out_ref[s, :, :WIDTH] = cache_ref[ids[s]]
        out_ref[s, :, DOWN_AT:] = down[row : row + 16, col : col + 128]


def serve(ids, cache_piece, info, saved, mark):
    return pl.pallas_call(
        serve_kernel,
        in_specs=[smem()] + [vmem()] * 4,
        out_specs=vmem(),
        out_shape=jax.ShapeDtypeStruct((NCTX, PIECE, SLOT_LANES), bf16),
        compiler_params=params(36),
        cost_estimate=cost(SERVE_FLOPS, 2e6),
    )(ids, cache_piece, info, saved, mark)


def up_kernel(info, g_ref, mark, up_out, rows_all):
    for s in range(NCTX):
        rows_all[0:16, s * 128 : (s + 1) * 128] = info[s, :, 256:384]
        rows_all[16:32, s * 128 : (s + 1) * 128] = info[s, :, 384:512]
    up_out[...] = mm(rows_all[...], g_ref[...], NT).astype(bf16)


def up_partial(info, g_t, mark):
    return pl.pallas_call(
        up_kernel,
        in_specs=[vmem()] * 3,
        out_specs=vmem(),
        out_shape=jax.ShapeDtypeStruct((RANK, FEATS), bf16),
        scratch_shapes=[pltpu.VMEM((RANK, NCTX * QRY_DEV), bf16)],
        compiler_params=params(36),
        cost_estimate=cost(1e8, 3e6),
    )(info, g_t, mark)


def gather_tp(own):
    pieces = [None] * NTP
    pieces[0] = own
    forward = own
    back = own
    for step in range(1, 5):
        forward = shift(forward, "tp", NTP, -1)
        pieces[step] = forward
        if step < 4:
            back = shift(back, "tp", NTP, 1)
            pieces[NTP - step] = back
    return pieces


def attend_kernel(place, *refs):
    pieces = refs[:NTP]
    q_ref, vu_ref, bias_ref, hg_mine, hg_other = refs[NTP : NTP + 5]
    dq_ref, up_ref = refs[NTP + 5 : NTP + 7]
    outs = refs[NTP + 7 : 2 * NTP + 7]
    keys, keys_t, spread, ds_all, p_all, q_all, og_all = refs[2 * NTP + 7 :]
    span = GSLOTS * PIECE
    lanes = 4 * GQ
    for g in range(GROUPS):
        for d in range(NTP):
            keys[g, d * span : (d + 1) * span, :] = pieces[d][g * span : (g + 1) * span, :]
    spread[...] = jnp.zeros_like(spread)
    base = SLOTS * PIECE
    total = pieces[0][base : base + 16, :512].astype(f32)
    for d in range(1, NTP):
        total = total + pieces[d][base : base + 16, :512].astype(f32)
    up_ref[:16, :] = ADAPTER_SCALE * total[:, :FEATS]
    up_ref[16:, :] = ADAPTER_SCALE * total[:, 256 : 256 + FEATS]

    def products(quad):
        here = slice(quad * lanes, (quad + 1) * lanes)
        at = slice((quad % 2) * 4 * VALUE, (quad % 2 + 1) * 4 * VALUE)
        hg = jnp.where(quad // 2 == place[2], hg_mine[:, at], hg_other[:, at])
        maps = jnp.concatenate([vu_ref[4 * quad + h] for h in range(4)], axis=1)
        raw = []
        for g in range(GROUPS):
            q4 = jnp.concatenate(
                [q_ref[4 * quad + h][:, g * GQ : (g + 1) * GQ] for h in range(4)], axis=1
            )
            for h in range(4):
                cols = slice(h * VALUE, (h + 1) * VALUE)
                spread[quad % 2, g, h * GQ : (h + 1) * GQ, cols] = hg[g * GQ : (g + 1) * GQ, cols]
            og = mm(maps, spread[quad % 2, g], NT).astype(bf16)
            q_all[g, :, here] = q4
            og_all[g, :, here] = og
            raw.append((mm(keys[g], q4, NN), mm(keys[g, :, :LATENT], og, NN)))
        return raw

    def softmax(quad, raw):
        here = slice(quad * lanes, (quad + 1) * lanes)
        dqs = []
        for g in range(GROUPS):
            s, dp = raw[g]
            s = s.reshape(NTP, GSLOTS, PIECE, lanes) * EXP2_SCALE + bias_ref[g][None, :, None, :]
            s = s.reshape(GROUP_ROWS, lanes)
            e = jnp.exp2(s - jnp.max(s, axis=0, keepdims=True))
            share = 1.0 / jnp.sum(e, axis=0, keepdims=True)
            delta = jnp.sum(e * dp, axis=0, keepdims=True) * share
            ds = (e * ((dp - delta) * (share * SCORE_SCALE))).astype(bf16)
            p_all[g, :, here] = (e * share).astype(bf16)
            ds_all[g, :, here] = ds
            dqs.append(mm(keys_t[g], ds, NN).astype(bf16))
        for h in range(4):
            cols = slice(h * GQ, (h + 1) * GQ)
            dq_ref[4 * quad + h] = jnp.concatenate([dqs[0][:, cols], dqs[1][:, cols]], axis=1)

    raw = products(0)
    for g in range(GROUPS):
        keys_t[g] = keys[g].T
    for quad in range(QUADS):
        later = products(quad + 1) if quad + 1 < QUADS else None
        softmax(quad, raw)
        raw = later
    for g in range(GROUPS):
        grads = mm(ds_all[g], q_all[g], NT)
        latent = grads[:, :LATENT] + mm(p_all[g], og_all[g], NT)
        latent = latent.astype(bf16)
        rope = grads[:, LATENT:].astype(bf16)
        for d in range(NTP):
            at = slice(g * span, (g + 1) * span)
            outs[d][at, :LATENT] = latent[d * span : (d + 1) * span]
            outs[d][at, LATENT:] = rope[d * span : (d + 1) * span]


def attend(place, pieces, q_t, vu, bias, hg_mine, hg_other):
    span = GSLOTS * PIECE
    rows = [2 * span] * NTP
    out_shape = [
        jax.ShapeDtypeStruct((HEADS_DEV, WIDTH, QRY_DEV), bf16),
        jax.ShapeDtypeStruct((RANK, FEATS), f32),
    ]
    out_shape += [jax.ShapeDtypeStruct((n, WIDTH), bf16) for n in rows]
    width = HEADS_DEV * GQ
    return pl.pallas_call(
        attend_kernel,
        in_specs=[smem()] + [vmem()] * (NTP + 5),
        out_specs=[vmem()] * (NTP + 2),
        out_shape=out_shape,
        scratch_shapes=[
            pltpu.VMEM((GROUPS, GROUP_ROWS, WIDTH), bf16),
            pltpu.VMEM((GROUPS, WIDTH, GROUP_ROWS), bf16),
            pltpu.VMEM((2, GROUPS, 4 * GQ, 4 * VALUE), bf16),
            pltpu.VMEM((GROUPS, GROUP_ROWS, width), bf16),
            pltpu.VMEM((GROUPS, GROUP_ROWS, width), bf16),
            pltpu.VMEM((GROUPS, WIDTH, width), bf16),
            pltpu.VMEM((GROUPS, LATENT, width), bf16),
        ],
        compiler_params=params(ATTEND_MIB),
        cost_estimate=cost(1e10, 1.2e7),
    )(place, *pieces, q_t, vu, bias, hg_mine, hg_other)


def reduce_tp(parts):
    up = shift(parts[4], "tp", NTP, 1)
    down = shift(parts[5], "tp", NTP, -1)
    up = shift(add(parts[3], up), "tp", NTP, 1)
    down = shift(add(parts[6], down), "tp", NTP, -1)
    up = shift(add(parts[2], up), "tp", NTP, 1)
    down = shift(add(parts[7], down), "tp", NTP, -1)
    up = shift(add(parts[1], up), "tp", NTP, 1)
    return parts[0], up, down


def slots_kernel(chosen, own, up, down, sums, out_ref):
    total = own[...].astype(f32) + up[...].astype(f32) + down[...].astype(f32)
    total = total.astype(bf16)
    empty = jnp.zeros((PIECE, WIDTH), bf16)
    for s in range(NCTX):
        out_ref[s, :, :WIDTH] = empty
        out_ref[s, :, DOWN_AT:] = sums[...]
    for k in range(SLOTS):
        out_ref[chosen[k], :, :WIDTH] = total[k * PIECE : (k + 1) * PIECE, :]


def to_slots(chosen, own, up, down, sums):
    return pl.pallas_call(
        slots_kernel,
        in_specs=[smem()] + [vmem()] * 4,
        out_specs=vmem(),
        out_shape=jax.ShapeDtypeStruct((NCTX, PIECE, SLOT_LANES), bf16),
        compiler_params=params(36),
        cost_estimate=cost(1e6, 2e6),
    )(chosen, own, up, down, sums)


def collect_kernel(ids, got_ref, out_ref, down_ref):
    out_ref[...] = jnp.zeros_like(out_ref)
    for s in range(NCTX):
        row, col = 16 * (s // 16), 128 * (s % 16)
        down_ref[row : row + 16, col : col + 128] = got_ref[s, :, DOWN_AT:].astype(f32)
        out_ref[ids[s]] += got_ref[s, :, :WIDTH].astype(f32)


def collect(ids, got, blocks):
    return pl.pallas_call(
        collect_kernel,
        in_specs=[smem(), vmem()],
        out_specs=[vmem(), vmem()],
        out_shape=[
            jax.ShapeDtypeStruct((blocks, PIECE, WIDTH), f32),
            jax.ShapeDtypeStruct((RANK, HEAD_IN), f32),
        ],
        compiler_params=params(36),
        cost_estimate=cost(1e6, 2e6),
    )(ids, got)


def shards(
    queries,
    latent_block_cache,
    selected_block_lists,
    output_gradient,
    output_weight,
    adapter_down,
    adapter_up,
    value_up_map,
    saved_head_input,
):
    ctx_axes = ("x", "y", "core")
    blocks_dev = latent_block_cache.shape[0]
    place = jnp.stack(
        [lax.axis_index("x"), lax.axis_index("y"), lax.axis_index("core"), lax.axis_index("tp")]
    ).astype(jnp.int32)

    holder = selected_block_lists // blocks_dev
    local = selected_block_lists - holder * blocks_dev
    every = jnp.arange(NCTX, dtype=jnp.int32)
    hit = holder[:, :, None] == every[None, None, :]
    wanted = jnp.max(jnp.where(hit, local[:, :, None], 0), axis=(0, 1))
    g_t = output_gradient.T
    mine, info, w_own, w_other, cache_piece = prep(
        place,
        wanted,
        g_t,
        adapter_up,
        output_weight.T,
        adapter_down,
        saved_head_input,
        jnp.swapaxes(latent_block_cache, 1, 2),
    )
    theirs = shift(mine, "core", 2, 1)
    w_pair = shift(w_other, "core", 2, 1)
    info = lax.all_to_all(info, ctx_axes, split_axis=0, concat_axis=0, tiled=True)

    used = jnp.any(hit.reshape(GROUPS, GQ * hit.shape[1], NCTX), axis=1).astype(jnp.int32)
    rank = jnp.cumsum(used, axis=1)
    slot_hit = (used[:, None, :] == 1) & (
        rank[:, None, :] == jnp.arange(1, GSLOTS + 1, dtype=jnp.int32)[None, :, None]
    )
    chosen = jnp.sum(jnp.where(slot_hit, every[None, None, :], 0), axis=2).reshape(SLOTS)
    holder_groups = holder.reshape(GROUPS, GQ, holder.shape[1])
    picked = jnp.any(
        holder_groups[:, None, :, :] == chosen.reshape(GROUPS, GSLOTS)[:, :, None, None], axis=3
    )
    bias = jnp.where(picked, 0.0, MASKED).astype(f32)
    bias = jnp.concatenate([bias] * 4, axis=2)

    own, p1, m1, p2, m2, mark = head_partials(place, mine, theirs, w_own, w_pair)
    ids = jnp.max(info[:, :8, 512:].astype(f32) + mark[None], axis=(1, 2)).astype(jnp.int32)
    minus = ring(p1, 0, 1)
    plus = ring(m1, 0, -1)

    slots = serve(ids, cache_piece, info, saved_head_input, mark)
    got = lax.all_to_all(slots, ctx_axes, split_axis=0, concat_axis=0, tiled=True)
    up_part = up_partial(info, g_t, mark)
    piece, down_sums = pick(chosen, got, up_part)
    pieces = gather_tp(piece)
    p2, m2 = relay(p2, m2, minus, plus, pieces[1])
    last_minus = ring(p2, 0, 1)
    last_plus = ring(m2, 0, -1)
    sums = corner(own, minus, plus, last_minus, last_plus, pieces[2], pieces[6])
    hg_mine, hg_other = total(place, sums[0], *[ring(sums[i], 1, i) for i in (1, 2, 3)])
    hg_other = shift(hg_other, "core", 2, 1)

    dq_t, up_gradient, *parts = attend(
        place,
        pieces,
        jnp.transpose(queries, (1, 2, 0)),
        value_up_map,
        bias,
        hg_mine,
        hg_other,
    )
    query_grads = jnp.transpose(dq_t, (2, 0, 1))

    own, up, down = reduce_tp(parts)
    slots = to_slots(chosen, own, up, down, down_sums)
    returned = lax.all_to_all(slots, ctx_axes, split_axis=0, concat_axis=0, tiled=True)
    cache_grads, down_gradient = collect(ids, returned, blocks_dev)
    return (query_grads, cache_grads, down_gradient, up_gradient)


def solution(mesh):
    split = Mesh(mesh.devices.reshape(NX, NY, NCORE, NTP), ("x", "y", "core", "tp"))
    ctx = ("x", "y", "core")
    placed = (
        P(ctx, "tp", None),
        P(ctx, None, None),
        P(ctx, None),
        P(None, ctx),
        P("tp", ctx),
        P(None, "tp"),
        P(None, ctx),
        P("tp", None, None),
        P(ctx, "tp"),
    )
    return jax.shard_map(
        shards,
        mesh=split,
        in_specs=placed,
        out_specs=(P(ctx, "tp", None), P(ctx, "tp", None), P(None, "tp"), P(None, ctx)),
        check_vma=False,
    )
```

```python
import functools

import jax
import jax.numpy as jnp
from jax import lax
from jax.experimental import pallas as pl
from jax.experimental.pallas import tpu as pltpu
from jax.sharding import Mesh, PartitionSpec as P

SCORE_SCALE = 192.0 ** (-0.5)
ADAPTER_SCALE = 2.0
EXP2_SCALE = SCORE_SCALE * 1.4426950408889634

NX = 4
NY = 4
NCORE = 2
NCTX = 32
NTP = 8
GROUPS = 2
GSLOTS = 6
SLOTS = 12
BLOCK = 128
WIDTH = 576
LATENT = 512
VALUE = 128
HEADS_DEV = 16
QRY_DEV = 128
GQ = 64
RANK = 32
FEATS = 224
HEAD_IN = 2048
HALF_IN = 1024
CHIP_QRY = 256
PIECE = BLOCK // NTP
INFO_LANES = 640
SLOT_LANES = 768
DOWN_AT = 640
PREP_PAIRS = 8
QUADS = 4
ATTEND_MIB = 34
HEAD_CUTS = 2
RING_COLS = 2
CORNER_FLOPS = 1e7
PICK_FLOPS = 1e11
SERVE_FLOPS = 1e6
GROUP_ROWS = GSLOTS * BLOCK
MASKED = -1e30

bf16 = jnp.bfloat16
f32 = jnp.float32

NN = (((1,), (0,)), ((), ()))
NT = (((1,), (1,)), ((), ()))
TN = (((0,), (0,)), ((), ()))


def mm(a, b, dims):
    return lax.dot_general(a, b, dims, preferred_element_type=f32)


def params(mib):
    return pltpu.CompilerParams(vmem_limit_bytes=mib * 1024 * 1024)


def cost(flops, nbytes):
    return pl.CostEstimate(flops=int(flops), bytes_accessed=int(nbytes), transcendentals=0)


def smem():
    return pl.BlockSpec(memory_space=pltpu.SMEM)


def vmem():
    return pl.BlockSpec(memory_space=pltpu.VMEM)


def prep_kernel(
    place,
    ids,
    g_ref,
    up_ref,
    w_ref,
    down_ref,
    saved_ref,
    cache_ref,
    rows_out,
    info,
    w_mine,
    w_other,
    cache_out,
    wcat,
    rows_t,
    block,
):
    step = pl.program_id(0)
    core = place[2]

    @pl.when(step == 0)
    def _():
        wcat[:FEATS, :] = w_ref[...]
        wcat[FEATS:, :] = (ADAPTER_SCALE * down_ref[...].astype(f32)).astype(bf16)
        w_mine[...] = wcat[:, pl.ds(pl.multiple_of(core * HALF_IN, HALF_IN), HALF_IN)]
        w_other[...] = wcat[:, pl.ds(pl.multiple_of((1 - core) * HALF_IN, HALF_IN), HALF_IN)]
        rows_t[...] = mm(down_ref[...], saved_ref[...], NT).astype(bf16)

    rows = rows_t[...]
    start = pl.multiple_of(place[3] * PIECE, PIECE)
    for pair in range(PREP_PAIRS):
        block[pair] = cache_ref[pair].T
        cache_out[pair] = block[pair, pl.ds(start, PIECE), :]
        g = g_ref[:, pair * 2 * QRY_DEV : (pair + 1) * 2 * QRY_DEV]
        low = mm(up_ref[...], g, NN).astype(bf16)
        rows_out[pair] = jnp.concatenate([g, low], axis=0).T
        for half in range(2):
            cols = slice(half * QRY_DEV, (half + 1) * QRY_DEV)
            at = 2 * pair + half
            info[at, :, 0:128] = low[:16, cols]
            info[at, :, 128:256] = low[16:, cols]
            info[at, :, 256:384] = rows[:16]
            info[at, :, 384:512] = rows[16:]
            number = ids[2 * PREP_PAIRS * step + at].astype(f32)
            info[at, :, 512:640] = jnp.full((16, 128), number, f32).astype(bf16)


def prep(place, ids, g_t, up, w_t, down, saved, cache_t):
    pairs = NX * NY
    blocks = cache_t.shape[0]
    step_blocks = blocks * PREP_PAIRS // pairs
    fixed = lambda s, p, i: (0, 0)
    moving = lambda s, p, i: (s, 0, 0)
    return pl.pallas_call(
        prep_kernel,
        grid_spec=pltpu.PrefetchScalarGridSpec(
            num_scalar_prefetch=2,
            grid=(pairs // PREP_PAIRS,),
            in_specs=[
                pl.BlockSpec((FEATS, PREP_PAIRS * 2 * QRY_DEV), lambda s, p, i: (0, s)),
                pl.BlockSpec((RANK, FEATS), fixed),
                pl.BlockSpec((FEATS, HEAD_IN), fixed),
                pl.BlockSpec((RANK, HEAD_IN), fixed),
                pl.BlockSpec((QRY_DEV, HEAD_IN), fixed),
                pl.BlockSpec((step_blocks, WIDTH, BLOCK), moving),
            ],
            out_specs=[
                pl.BlockSpec((PREP_PAIRS, 256, 256), moving),
                pl.BlockSpec((2 * PREP_PAIRS, 16, INFO_LANES), moving),
                pl.BlockSpec((256, HALF_IN), fixed),
                pl.BlockSpec((256, HALF_IN), fixed),
                pl.BlockSpec((step_blocks, PIECE, WIDTH), moving),
            ],
            scratch_shapes=[
                pltpu.VMEM((256, HEAD_IN), bf16),
                pltpu.VMEM((RANK, QRY_DEV), bf16),
                pltpu.VMEM((step_blocks, BLOCK, WIDTH), bf16),
            ],
        ),
        out_shape=[
            jax.ShapeDtypeStruct((pairs, 256, 256), bf16),
            jax.ShapeDtypeStruct((NCTX, 16, INFO_LANES), bf16),
            jax.ShapeDtypeStruct((256, HALF_IN), bf16),
            jax.ShapeDtypeStruct((256, HALF_IN), bf16),
            jax.ShapeDtypeStruct((blocks, PIECE, WIDTH), bf16),
        ],
        compiler_params=params(60),
        cost_estimate=cost(1e8, 6e6),
    )(place, ids, g_t, up, w_t, down, saved, cache_t)


def head_kernel(place, *refs):
    mine, theirs = refs[0:4], refs[4:8]
    w_own, w_pair = refs[8:10]
    (own, p1, m1, p2, m2, mark) = refs[10:]
    step = pl.program_id(0)
    rows = jnp.concatenate(
        [jnp.concatenate([m[0], t[0]], axis=1) for m, t in zip(mine, theirs)], axis=0
    )
    mark[...] = jnp.zeros_like(mark)
    steps = [
        [(own, 0), (own, 1), (own, 2), (own, 3)],
        [(p2, 0), (p2, 1), (p1, 0), (p1, 1)],
        [(p1, 0), (p1, 1), (m1, 0), (m1, 1)],
        [(m1, 0), (m1, 1), (m2, 0), (m2, 1)],
    ]
    for d1, places in enumerate(steps):

        @pl.when(step == d1)
        def _(places=places):
            for cut in range(HEAD_CUTS):
                size = HALF_IN // HEAD_CUTS
                cols = slice(cut * size, (cut + 1) * size)
                w = jnp.concatenate([w_own[:, cols], w_pair[:, cols]], axis=0)
                both = mm(rows, w, NN).astype(bf16)
                for d2, (ref, at) in enumerate(places):
                    ref[at, :, cols] = both[CHIP_QRY * d2 : CHIP_QRY * (d2 + 1)]


def head_partials(place, mine, theirs, w_own, w_pair):
    def row(d2):
        def index(s, p):
            on_x = jnp.where(p[2] == 0, s, d2)
            on_y = jnp.where(p[2] == 0, d2, s)
            return (lax.rem(p[0] + on_x, NX) * NY + lax.rem(p[1] + on_y, NY), 0, 0)

        return pl.BlockSpec((1, CHIP_QRY, 256), index)

    def whole():
        return pl.BlockSpec((256, HALF_IN), lambda s, p: (0, 0))

    def past(s, bound):
        return (s > bound).astype(jnp.int32)

    def out(count, block, index):
        return (
            pl.BlockSpec((block, CHIP_QRY, HALF_IN), lambda s, p: (index(s), 0, 0)),
            jax.ShapeDtypeStruct((count, CHIP_QRY, HALF_IN), bf16),
        )

    outs = [
        out(4, 4, lambda s: 0),
        out(4, 2, lambda s: past(s, 1)),
        out(4, 2, lambda s: past(s, 2)),
        out(2, 2, lambda s: 0),
        out(2, 2, lambda s: 0),
        (
            pl.BlockSpec((8, 128), lambda s, p: (0, 0)),
            jax.ShapeDtypeStruct((8, 128), f32),
        ),
    ]
    return pl.pallas_call(
        head_kernel,
        grid_spec=pltpu.PrefetchScalarGridSpec(
            num_scalar_prefetch=1,
            grid=(4,),
            in_specs=[row(i) for i in range(4)] * 2 + [whole(), whole()],
            out_specs=[o[0] for o in outs],
        ),
        out_shape=[o[1] for o in outs],
        compiler_params=params(60),
        cost_estimate=cost(4.3e9, 13e6),
    )(place, *[mine] * 4, *[theirs] * 4, w_own, w_pair)


def ring(value, order, by):
    pairs = []
    for x in range(NX):
        for y in range(NY):
            for core in range(NCORE):
                if core == order:
                    to = ((x + by) % NX, y)
                else:
                    to = (x, (y + by) % NY)
                pairs.append(((x * NY + y) * 2 + core, (to[0] * NY + to[1]) * 2 + core))
    return lax.ppermute(value, ("x", "y", "core"), pairs)


def shift(value, axis, size, by):
    return lax.ppermute(value, axis, [(i, (i + by) % size) for i in range(size)])


def add(*terms):
    total = terms[0].astype(f32)
    for t in terms[1:]:
        total = total + t.astype(f32)
    return total.astype(bf16)


def call_whole(kernel, outs, mib, flops, nbytes, *args):
    return pl.pallas_call(
        kernel,
        in_specs=[vmem()] * len(args),
        out_specs=[vmem()] * len(outs),
        out_shape=[jax.ShapeDtypeStruct(o, bf16) for o in outs],
        compiler_params=params(mib),
        cost_estimate=cost(flops, nbytes),
    )(*args)


def relay_kernel(p, m, minus, plus, mark, o1, o2):
    o1[...] = add(p[...], minus[...])
    o2[...] = add(m[...], plus[...])


def columns(count, rest, at=0):
    block = (count,) + rest + (HALF_IN // RING_COLS,)
    if rest:
        return pl.BlockSpec(block, lambda s: (at, 0, s))
    return pl.BlockSpec(block, lambda s: (0, s))


def relay(*args):
    return pl.pallas_call(
        relay_kernel,
        grid=(RING_COLS,),
        in_specs=[columns(2, (CHIP_QRY,), at) for at in (0, 0, 1, 0)]
        + [pl.BlockSpec((16, 128), lambda s: (0, 0))],
        out_specs=[columns(2, (CHIP_QRY,))] * 2,
        out_shape=[jax.ShapeDtypeStruct((2, CHIP_QRY, HALF_IN), bf16)] * 2,
        compiler_params=params(12),
        cost_estimate=cost(1e7, 6e6),
    )(*args)


def corner_kernel(own, minus, plus, last_minus, last_plus, mark_a, mark_b, *outs):
    for i in range(2):
        outs[i][...] = add(own[i], plus[i], last_minus[i])
        outs[2 + i][...] = add(own[2 + i], minus[i], last_plus[i])


def corner(*args):
    two = columns(2, (CHIP_QRY,))
    return pl.pallas_call(
        corner_kernel,
        grid=(RING_COLS,),
        in_specs=[columns(4, (CHIP_QRY,)), two, columns(2, (CHIP_QRY,), 1), two, two]
        + [pl.BlockSpec((16, 128), lambda s: (0, 0))] * 2,
        out_specs=[columns(CHIP_QRY, ())] * 4,
        out_shape=[jax.ShapeDtypeStruct((CHIP_QRY, HALF_IN), bf16)] * 4,
        compiler_params=params(16),
        cost_estimate=cost(1e7, 8e6),
    )(*args)


def total_kernel(place, a, b, c, d, mine, other):
    core = place[2]
    here = pl.ds(pl.multiple_of(core * QRY_DEV, QRY_DEV), QRY_DEV)
    there = pl.ds(pl.multiple_of((1 - core) * QRY_DEV, QRY_DEV), QRY_DEV)
    mine[...] = add(a[here, :], b[here, :], c[here, :], d[here, :])
    other[...] = add(a[there, :], b[there, :], c[there, :], d[there, :])


def total(place, *args):
    return pl.pallas_call(
        total_kernel,
        in_specs=[smem()] + [vmem()] * 4,
        out_specs=[vmem()] * 2,
        out_shape=[jax.ShapeDtypeStruct((QRY_DEV, HALF_IN), bf16)] * 2,
        compiler_params=params(8),
        cost_estimate=cost(1e6, 3e6),
    )(place, *args)


def pick_kernel(chosen, got, up_ref, piece, down_out):
    for k in range(SLOTS):
        piece[k * PIECE : (k + 1) * PIECE, :] = got[chosen[k], :, :WIDTH]
    base = SLOTS * PIECE
    piece[base : base + 16, :] = jnp.zeros((16, WIDTH), bf16)
    piece[base : base + 16, :FEATS] = up_ref[:16]
    piece[base : base + 16, 256 : 256 + FEATS] = up_ref[16:]
    down = got[0, :, DOWN_AT:].astype(f32)
    for s in range(1, NCTX):
        down = down + got[s, :, DOWN_AT:].astype(f32)
    down_out[...] = down.astype(bf16)


def pick(chosen, got, up):
    outs = [(SLOTS * PIECE + 16, WIDTH), (16, 128)]
    return pl.pallas_call(
        pick_kernel,
        in_specs=[smem(), vmem(), vmem()],
        out_specs=[vmem()] * 2,
        out_shape=[jax.ShapeDtypeStruct(o, bf16) for o in outs],
        compiler_params=params(8),
        cost_estimate=cost(PICK_FLOPS, 1e6),
    )(chosen, got, up)


def serve_kernel(ids, cache_ref, info, saved_ref, mark, out_ref):
    low0 = info[0, :, 0:128].astype(f32)
    low1 = info[0, :, 128:256].astype(f32)
    for s in range(1, NCTX):
        low0 = low0 + info[s, :, 0:128].astype(f32)
        low1 = low1 + info[s, :, 128:256].astype(f32)
    low = (ADAPTER_SCALE * jnp.concatenate([low0, low1], axis=0)).astype(bf16)
    down = mm(low, saved_ref[...], NN).astype(bf16)
    for s in range(NCTX):
        row, col = 16 * (s // 16), 128 * (s % 16)
        out_ref[s, :, :WIDTH] = cache_ref[ids[s]]
        out_ref[s, :, DOWN_AT:] = down[row : row + 16, col : col + 128]


def serve(ids, cache_piece, info, saved, mark):
    return pl.pallas_call(
        serve_kernel,
        in_specs=[smem()] + [vmem()] * 4,
        out_specs=vmem(),
        out_shape=jax.ShapeDtypeStruct((NCTX, PIECE, SLOT_LANES), bf16),
        compiler_params=params(8),
        cost_estimate=cost(SERVE_FLOPS, 2e6),
    )(ids, cache_piece, info, saved, mark)


def up_kernel(info, g_ref, mark, up_out, rows_all):
    for s in range(NCTX):
        rows_all[0:16, s * 128 : (s + 1) * 128] = info[s, :, 256:384]
        rows_all[16:32, s * 128 : (s + 1) * 128] = info[s, :, 384:512]
    up_out[...] = mm(rows_all[...], g_ref[...], NT).astype(bf16)


def up_partial(info, g_t, mark):
    return pl.pallas_call(
        up_kernel,
        in_specs=[vmem()] * 3,
        out_specs=vmem(),
        out_shape=jax.ShapeDtypeStruct((RANK, FEATS), bf16),
        scratch_shapes=[pltpu.VMEM((RANK, NCTX * QRY_DEV), bf16)],
        compiler_params=params(10),
        cost_estimate=cost(1e8, 3e6),
    )(info, g_t, mark)


def gather_tp(own):
    pieces = [None] * NTP
    pieces[0] = own
    forward = own
    back = own
    for step in range(1, 5):
        forward = shift(forward, "tp", NTP, -1)
        pieces[step] = forward
        if step < 4:
            back = shift(back, "tp", NTP, 1)
            pieces[NTP - step] = back
    return pieces


def attend_kernel(place, *refs):
    pieces = refs[:NTP]
    q_ref, vu_ref, bias_ref, hg_mine, hg_other = refs[NTP : NTP + 5]
    dq_ref, up_ref = refs[NTP + 5 : NTP + 7]
    outs = refs[NTP + 7 : 2 * NTP + 7]
    keys, keys_t, spread, ds_all, p_all, q_all, og_all = refs[2 * NTP + 7 :]
    span = GSLOTS * PIECE
    lanes = 4 * GQ
    for g in range(GROUPS):
        for d in range(NTP):
            keys[g, d * span : (d + 1) * span, :] = pieces[d][g * span : (g + 1) * span, :]
    spread[...] = jnp.zeros_like(spread)
    base = SLOTS * PIECE
    total = pieces[0][base : base + 16, :512].astype(f32)
    for d in range(1, NTP):
        total = total + pieces[d][base : base + 16, :512].astype(f32)
    up_ref[:16, :] = ADAPTER_SCALE * total[:, :FEATS]
    up_ref[16:, :] = ADAPTER_SCALE * total[:, 256 : 256 + FEATS]

    def products(quad):
        here = slice(quad * lanes, (quad + 1) * lanes)
        at = slice((quad % 2) * 4 * VALUE, (quad % 2 + 1) * 4 * VALUE)
        hg = jnp.where(quad // 2 == place[2], hg_mine[:, at], hg_other[:, at])
        maps = jnp.concatenate([vu_ref[4 * quad + h] for h in range(4)], axis=1)
        raw = []
        for g in range(GROUPS):
            q4 = jnp.concatenate(
                [q_ref[4 * quad + h][:, g * GQ : (g + 1) * GQ] for h in range(4)], axis=1
            )
            for h in range(4):
                cols = slice(h * VALUE, (h + 1) * VALUE)
                spread[quad % 2, g, h * GQ : (h + 1) * GQ, cols] = hg[g * GQ : (g + 1) * GQ, cols]
            og = mm(maps, spread[quad % 2, g], NT).astype(bf16)
            q_all[g, :, here] = q4
            og_all[g, :, here] = og
            raw.append((mm(keys[g], q4, NN), mm(keys[g, :, :LATENT], og, NN)))
        return raw

    def softmax(quad, raw):
        here = slice(quad * lanes, (quad + 1) * lanes)
        dqs = []
        for g in range(GROUPS):
            s, dp = raw[g]
            s = s.reshape(NTP, GSLOTS, PIECE, lanes) * EXP2_SCALE + bias_ref[g][None, :, None, :]
            s = s.reshape(GROUP_ROWS, lanes)
            e = jnp.exp2(s - jnp.max(s, axis=0, keepdims=True))
            share = 1.0 / jnp.sum(e, axis=0, keepdims=True)
            delta = jnp.sum(e * dp, axis=0, keepdims=True) * share
            ds = (e * ((dp - delta) * (share * SCORE_SCALE))).astype(bf16)
            p_all[g, :, here] = (e * share).astype(bf16)
            ds_all[g, :, here] = ds
            dqs.append(mm(keys_t[g], ds, NN).astype(bf16))
        for h in range(4):
            cols = slice(h * GQ, (h + 1) * GQ)
            dq_ref[4 * quad + h] = jnp.concatenate([dqs[0][:, cols], dqs[1][:, cols]], axis=1)

    raw = products(0)
    for g in range(GROUPS):
        keys_t[g] = keys[g].T
    for quad in range(QUADS):
        later = products(quad + 1) if quad + 1 < QUADS else None
        softmax(quad, raw)
        raw = later
    for g in range(GROUPS):
        grads = mm(ds_all[g], q_all[g], NT)
        latent = grads[:, :LATENT] + mm(p_all[g], og_all[g], NT)
        latent = latent.astype(bf16)
        rope = grads[:, LATENT:].astype(bf16)
        for d in range(NTP):
            at = slice(g * span, (g + 1) * span)
            outs[d][at, :LATENT] = latent[d * span : (d + 1) * span]
            outs[d][at, LATENT:] = rope[d * span : (d + 1) * span]


def attend(place, pieces, q_t, vu, bias, hg_mine, hg_other):
    span = GSLOTS * PIECE
    rows = [2 * span] * NTP
    out_shape = [
        jax.ShapeDtypeStruct((HEADS_DEV, WIDTH, QRY_DEV), bf16),
        jax.ShapeDtypeStruct((RANK, FEATS), f32),
    ]
    out_shape += [jax.ShapeDtypeStruct((n, WIDTH), bf16) for n in rows]
    width = HEADS_DEV * GQ
    return pl.pallas_call(
        attend_kernel,
        in_specs=[smem()] + [vmem()] * (NTP + 5),
        out_specs=[vmem()] * (NTP + 2),
        out_shape=out_shape,
        scratch_shapes=[
            pltpu.VMEM((GROUPS, GROUP_ROWS, WIDTH), bf16),
            pltpu.VMEM((GROUPS, WIDTH, GROUP_ROWS), bf16),
            pltpu.VMEM((2, GROUPS, 4 * GQ, 4 * VALUE), bf16),
            pltpu.VMEM((GROUPS, GROUP_ROWS, width), bf16),
            pltpu.VMEM((GROUPS, GROUP_ROWS, width), bf16),
            pltpu.VMEM((GROUPS, WIDTH, width), bf16),
            pltpu.VMEM((GROUPS, LATENT, width), bf16),
        ],
        compiler_params=params(ATTEND_MIB),
        cost_estimate=cost(1e10, 1.2e7),
    )(place, *pieces, q_t, vu, bias, hg_mine, hg_other)


def reduce_tp(parts):
    up = shift(parts[4], "tp", NTP, 1)
    down = shift(parts[5], "tp", NTP, -1)
    up = shift(add(parts[3], up), "tp", NTP, 1)
    down = shift(add(parts[6], down), "tp", NTP, -1)
    up = shift(add(parts[2], up), "tp", NTP, 1)
    down = shift(add(parts[7], down), "tp", NTP, -1)
    up = shift(add(parts[1], up), "tp", NTP, 1)
    return parts[0], up, down


def slots_kernel(chosen, own, up, down, sums, out_ref):
    total = own[...].astype(f32) + up[...].astype(f32) + down[...].astype(f32)
    total = total.astype(bf16)
    empty = jnp.zeros((PIECE, WIDTH), bf16)
    for s in range(NCTX):
        out_ref[s, :, :WIDTH] = empty
        out_ref[s, :, DOWN_AT:] = sums[...]
    for k in range(SLOTS):
        out_ref[chosen[k], :, :WIDTH] = total[k * PIECE : (k + 1) * PIECE, :]


def to_slots(chosen, own, up, down, sums):
    return pl.pallas_call(
        slots_kernel,
        in_specs=[smem()] + [vmem()] * 4,
        out_specs=vmem(),
        out_shape=jax.ShapeDtypeStruct((NCTX, PIECE, SLOT_LANES), bf16),
        compiler_params=params(8),
        cost_estimate=cost(1e6, 2e6),
    )(chosen, own, up, down, sums)


def collect_kernel(ids, got_ref, out_ref, down_ref):
    out_ref[...] = jnp.zeros_like(out_ref)
    for s in range(NCTX):
        row, col = 16 * (s // 16), 128 * (s % 16)
        down_ref[row : row + 16, col : col + 128] = got_ref[s, :, DOWN_AT:].astype(f32)
        out_ref[ids[s]] += got_ref[s, :, :WIDTH].astype(f32)


def collect(ids, got, blocks):
    return pl.pallas_call(
        collect_kernel,
        in_specs=[smem(), vmem()],
        out_specs=[vmem(), vmem()],
        out_shape=[
            jax.ShapeDtypeStruct((blocks, PIECE, WIDTH), f32),
            jax.ShapeDtypeStruct((RANK, HEAD_IN), f32),
        ],
        compiler_params=params(8),
        cost_estimate=cost(1e6, 2e6),
    )(ids, got)


def shards(
    queries,
    latent_block_cache,
    selected_block_lists,
    output_gradient,
    output_weight,
    adapter_down,
    adapter_up,
    value_up_map,
    saved_head_input,
):
    ctx_axes = ("x", "y", "core")
    blocks_dev = latent_block_cache.shape[0]
    place = jnp.stack(
        [lax.axis_index("x"), lax.axis_index("y"), lax.axis_index("core"), lax.axis_index("tp")]
    ).astype(jnp.int32)

    holder = selected_block_lists // blocks_dev
    local = selected_block_lists - holder * blocks_dev
    every = jnp.arange(NCTX, dtype=jnp.int32)
    hit = holder[:, :, None] == every[None, None, :]
    wanted = jnp.max(jnp.where(hit, local[:, :, None], 0), axis=(0, 1))
    g_t = output_gradient.T
    mine, info, w_own, w_other, cache_piece = prep(
        place,
        wanted,
        g_t,
        adapter_up,
        output_weight.T,
        adapter_down,
        saved_head_input,
        jnp.swapaxes(latent_block_cache, 1, 2),
    )
    theirs = shift(mine, "core", 2, 1)
    w_pair = shift(w_other, "core", 2, 1)
    info = lax.all_to_all(info, ctx_axes, split_axis=0, concat_axis=0, tiled=True)

    used = jnp.any(hit.reshape(GROUPS, GQ * hit.shape[1], NCTX), axis=1).astype(jnp.int32)
    rank = jnp.cumsum(used, axis=1)
    slot_hit = (used[:, None, :] == 1) & (
        rank[:, None, :] == jnp.arange(1, GSLOTS + 1, dtype=jnp.int32)[None, :, None]
    )
    chosen = jnp.sum(jnp.where(slot_hit, every[None, None, :], 0), axis=2).reshape(SLOTS)
    holder_groups = holder.reshape(GROUPS, GQ, holder.shape[1])
    picked = jnp.any(
        holder_groups[:, None, :, :] == chosen.reshape(GROUPS, GSLOTS)[:, :, None, None], axis=3
    )
    bias = jnp.where(picked, 0.0, MASKED).astype(f32)
    bias = jnp.concatenate([bias] * 4, axis=2)

    own, p1, m1, p2, m2, mark = head_partials(place, mine, theirs, w_own, w_pair)
    ids = jnp.max(info[:, :8, 512:].astype(f32) + mark[None], axis=(1, 2)).astype(jnp.int32)
    minus = ring(p1, 0, 1)
    plus = ring(m1, 0, -1)

    slots = serve(ids, cache_piece, info, saved_head_input, mark)
    got = lax.all_to_all(slots, ctx_axes, split_axis=0, concat_axis=0, tiled=True)
    up_part = up_partial(info, g_t, mark)
    piece, down_sums = pick(chosen, got, up_part)
    pieces = gather_tp(piece)
    p2, m2 = relay(p2, m2, minus, plus, pieces[1])
    last_minus = ring(p2, 0, 1)
    last_plus = ring(m2, 0, -1)
    sums = corner(own, minus, plus, last_minus, last_plus, pieces[2], pieces[7])
    hg_mine, hg_other = total(place, sums[0], *[ring(sums[i], 1, i) for i in (1, 2, 3)])
    hg_other = shift(hg_other, "core", 2, 1)

    dq_t, up_gradient, *parts = attend(
        place,
        pieces,
        jnp.transpose(queries, (1, 2, 0)),
        value_up_map,
        bias,
        hg_mine,
        hg_other,
    )
    query_grads = jnp.transpose(dq_t, (2, 0, 1))

    own, up, down = reduce_tp(parts)
    slots = to_slots(chosen, own, up, down, down_sums)
    returned = lax.all_to_all(slots, ctx_axes, split_axis=0, concat_axis=0, tiled=True)
    cache_grads, down_gradient = collect(ids, returned, blocks_dev)
    return (query_grads, cache_grads, down_gradient, up_gradient)


def solution(mesh):
    split = Mesh(mesh.devices.reshape(NX, NY, NCORE, NTP), ("x", "y", "core", "tp"))
    ctx = ("x", "y", "core")
    placed = (
        P(ctx, "tp", None),
        P(ctx, None, None),
        P(ctx, None),
        P(None, ctx),
        P("tp", ctx),
        P(None, "tp"),
        P(None, ctx),
        P("tp", None, None),
        P(ctx, "tp"),
    )
    return jax.shard_map(
        shards,
        mesh=split,
        in_specs=placed,
        out_specs=(P(ctx, "tp", None), P(ctx, "tp", None), P(None, "tp"), P(None, ctx)),
        check_vma=False,
    )
```
